256 devices in a mesh: shot: 16 (over y, x_lo, core), seq: 16 (over z, x_hi).
Axes of the slice: x: 4 (x_hi: 2, x_lo: 2; x = x_hi * 2 + x_lo), y: 4, z: 8, core: 2. Of those that a mesh axis runs over, the one named last changes fastest.
Arguments:
- query_rows: bfloat16 [16, 2048, 1536], P('shot', 'seq'), may hold values from -4.5188047 to 4.5188047
- key_rows: bfloat16 [16, 2048, 1536], P('shot', 'seq'), may hold values from -4.5188047 to 4.5188047
- value_rows: bfloat16 [16, 2048, 1536], P('shot', 'seq'), may hold values from -6 to 6
- out_grad: bfloat16 [16, 2048, 1536], P('shot', 'seq'), may hold values from -6 to 6
- shot_lengths: int32 [16], replicated, may hold values from 1024 to 2048, as said below
- global_positions: int32 [16, 16], P('shot'), may hold values from 0 to 2047, as said below
Outputs:
- attended: bfloat16 [16, 2048, 1536], P('shot', 'seq')
- query_grad: bfloat16 [16, 2048, 1536], P('shot', 'seq')
- key_grad: bfloat16 [16, 2048, 1536], P('shot', 'seq')
- value_grad: bfloat16 [16, 2048, 1536], P('shot', 'seq')
The draws below stay inside these ranges and needn't reach their ends.
Inputs may be any that keep to these rules, and one draw needn't show every extreme that they name: `shot_lengths`: in every draw one shot has 2048 tokens and another 2048 // 2. `global_positions`: in each shot, entries 1 * b to 1 * (b + 1) - 1 are distinct positions among rows 128 * b to 128 * (b + 1) - 1, for every b.
All inputs are finite; a program needn't handle non-finite values.
Results may differ from the reference program's by a relative error of at most 0.023.
Values may be sent and summed in bfloat16 or wider, within the bound.
A program may use at most 128 MiB of HBM per device.

```python
import math
import jax
import jax.numpy as jnp
from jax import lax

HEADS = 12
HEAD_DIM = 128
ROW_DEV = 128
GLOBAL_DEV = 1
ROWS = 2048
FEATURES = 1536
N_SHOT = 16


def draw_query_rows(key, part):
    key = jax.random.fold_in(key, 7)
    shape = (N_SHOT, ROWS, HEADS * HEAD_DIM)
    values = jnp.clip(jax.random.normal(key, shape, jnp.float32), -4.5, 4.5)
    return values.astype(jnp.bfloat16)


def draw_key_rows(key, part):
    key = jax.random.fold_in(key, 11)
    shape = (N_SHOT, ROWS, HEADS * HEAD_DIM)
    values = jnp.clip(jax.random.normal(key, shape, jnp.float32), -4.5, 4.5)
    return values.astype(jnp.bfloat16)


def draw_shot_lengths(key, part):
    key = jax.random.fold_in(key, 3)
    first, second, third = jax.random.split(key, 3)
    lengths = jax.random.randint(first, (N_SHOT,), ROWS // 2, ROWS + 1)
    full_shot = jax.random.randint(second, (), 0, N_SHOT)
    half_shot = (full_shot + 1 + jax.random.randint(third, (), 0, N_SHOT - 1)) % N_SHOT
    lengths = lengths.at[full_shot].set(ROWS).at[half_shot].set(ROWS // 2)
    return lengths.astype(jnp.int32)


def draw_global_positions(key, part):
    key = jax.random.fold_in(key, 5)
    blocks = ROWS // ROW_DEV
    keys = jax.random.split(key, N_SHOT * blocks)
    picks = jax.vmap(lambda sub: jax.random.permutation(sub, ROW_DEV)[:GLOBAL_DEV])(keys)
    offsets = jnp.arange(N_SHOT * blocks) % blocks * ROW_DEV
    return (picks + offsets[:, None]).reshape(N_SHOT, blocks * GLOBAL_DEV).astype(jnp.int32)


def spiked(entries, stream_key, source, target, shards_of, factor):
    owner, partner = [(jnp.arange(entries.shape[position]) // (entries.shape[position] // shards_of)).reshape([-1 if axis == position else 1 for axis in range(entries.ndim)]) for position in (source, target)]
    chosen = jax.random.permutation(stream_key, shards_of)[partner]
    strong = (owner == chosen) | (owner == (partner + shards_of // 2) % shards_of)
    return jnp.where(strong, factor * entries, entries)


def block_levels(own_key, dims, cuts, smallest, largest):
    def one(position, shards_of):
        steps = jax.random.uniform(jax.random.fold_in(jax.random.fold_in(own_key, 6), position), (shards_of,), jnp.float32, smallest / len(cuts), largest / len(cuts))
        return jnp.repeat(jnp.exp(steps), dims[position] // shards_of).reshape((-1,) + (1,) * (len(dims) - position - 1))

    factor_of = one(*cuts[0])
    for cut in cuts[1:]:
        factor_of = factor_of * one(*cut)
    return factor_of


def gaussian(key, shape, scale, bound, cuts=(), held_as=jnp.bfloat16):
    values = scale * jax.random.normal(key, shape, jnp.float32)
    if cuts:
        values = values * block_levels(key, shape, cuts, -0.22, 0.18)
    return jnp.clip(values, -bound, bound).astype(held_as)


def bell_draw_with(own_key, dims, spread, most, shards, heavy, kind=jnp.bfloat16):
    entries = spread * jax.random.normal(own_key, dims, jnp.float32)
    if shards:
        entries = entries * block_levels(own_key, dims, shards, -0.22, 0.18)
    return jnp.clip(spiked(entries, jax.random.fold_in(own_key, 3), *heavy), -most, most).astype(kind)


def setup_inputs(seed: int = 0) -> dict:
    arg_keys = jax.random.split(jax.random.key(seed), 7)
    return {
        "query_rows": draw_query_rows(jax.random.fold_in(arg_keys[6], 71), 0),
        "key_rows": draw_key_rows(jax.random.fold_in(arg_keys[6], 71), 0),
        "value_rows": gaussian(arg_keys[2], (N_SHOT, ROWS, FEATURES), 1.0, 6.0, ((0, 16), (1, 16))),
        "out_grad": bell_draw_with(arg_keys[3], (N_SHOT, ROWS, FEATURES), 1.0, 6.0, ((0, 16), (1, 16)), (0, 1, 16, 2.0)),
        "shot_lengths": draw_shot_lengths(jax.random.fold_in(arg_keys[6], 71), 0),
        "global_positions": draw_global_positions(jax.random.fold_in(arg_keys[6], 71), 0),
    }


NEG_FILL = -1e+30

def reference(query_rows, key_rows, value_rows, out_grad, shot_lengths, global_positions):
    shot_count, row_count, features = query_rows.shape
    glob_count = global_positions.shape[1]
    score_scale = 1.0 / math.sqrt(HEAD_DIM)
    query_heads = query_rows.reshape(shot_count, row_count, HEADS, HEAD_DIM)
    key_heads = key_rows.reshape(shot_count, row_count, HEADS, HEAD_DIM)
    value_heads = value_rows.reshape(shot_count, row_count, HEADS, HEAD_DIM)
    grad_heads = out_grad.reshape(shot_count, row_count, HEADS, HEAD_DIM)
    glob_keys = jax.vmap(lambda block, where_at: block[where_at])(key_heads, global_positions)
    glob_values = jax.vmap(lambda block, where_at: block[where_at])(value_heads, global_positions)
    glob_keys = glob_keys.reshape(shot_count * glob_count, HEADS, HEAD_DIM).astype(jnp.float32)
    glob_values = glob_values.reshape(shot_count * glob_count, HEADS, HEAD_DIM).astype(jnp.float32)
    glob_owner = jnp.arange(shot_count * glob_count, dtype=jnp.int32) // glob_count
    positions = jnp.arange(row_count, dtype=jnp.int32)

    def per_shot(shot_index):
        queries = query_heads[shot_index].astype(jnp.float32)
        grads = grad_heads[shot_index].astype(jnp.float32)
        is_global = jnp.any(positions[:, None] == global_positions[shot_index][None, :], axis=1)
        alive_mask = (positions < shot_lengths[shot_index]) | is_global
        cross_mask = glob_owner != shot_index
        all_keys = jnp.concatenate([key_heads[shot_index].astype(jnp.float32), glob_keys], axis=0)
        all_values = jnp.concatenate([value_heads[shot_index].astype(jnp.float32), glob_values], axis=0)
        used = jnp.concatenate([alive_mask, cross_mask], axis=0)
        logits = jnp.einsum('ihd,jhd->hij', queries, all_keys) * score_scale
        logits = jnp.where(used[None, None, :], logits, NEG_FILL)
        row_max = lax.optimization_barrier(jnp.max(logits, axis=-1))
        totals = lax.optimization_barrier(jnp.sum(jnp.where(used[None, None, :], jnp.exp(logits - row_max[..., None]), 0.0), axis=-1))
        row_lse = row_max + jnp.log(totals)
        weights = jnp.where(used[None, None, :], jnp.exp(logits - row_lse[..., None]), 0.0)
        weights_low = lax.optimization_barrier(weights.astype(jnp.bfloat16)).astype(jnp.float32)
        attended = jnp.einsum('hij,jhd->ihd', weights_low, all_values).astype(jnp.bfloat16)
        delta = lax.optimization_barrier(jnp.sum(grads * attended.astype(jnp.float32), axis=-1)).T
        dprod = jnp.einsum('ihd,jhd->hij', grads, all_values)
        dlogits = lax.optimization_barrier((weights * (dprod - delta[..., None])).astype(jnp.bfloat16)).astype(jnp.float32)
        query_grad = (score_scale * jnp.einsum('hij,jhd->ihd', dlogits, all_keys)).astype(jnp.bfloat16)
        key_part = score_scale * jnp.einsum('hij,ihd->jhd', dlogits, queries)
        value_part = jnp.einsum('hij,ihd->jhd', weights_low, grads)
        return (attended, query_grad, key_part[:row_count], value_part[:row_count], key_part[row_count:], value_part[row_count:])
    results = lax.map(per_shot, jnp.arange(shot_count, dtype=jnp.int32))
    attended, query_grad, key_local, value_local, key_cross, value_cross = results
    key_cross = lax.optimization_barrier(jnp.sum(key_cross, axis=0)).reshape(shot_count, glob_count, features)
    value_cross = lax.optimization_barrier(jnp.sum(value_cross, axis=0)).reshape(shot_count, glob_count, features)
    key_local = key_local.reshape(shot_count, row_count, features)
    value_local = value_local.reshape(shot_count, row_count, features)
    add_rows = jax.vmap(lambda block, where_at, extra: block.at[where_at].add(extra))
    key_grad = add_rows(key_local, global_positions, key_cross).astype(jnp.bfloat16)
    value_grad = add_rows(value_local, global_positions, value_cross).astype(jnp.bfloat16)
    return (attended.reshape(shot_count, row_count, features), query_grad.reshape(shot_count, row_count, features), key_grad, value_grad)
```

```python
import math

import jax
import jax.numpy as jnp
from jax import lax
from jax.experimental import pallas as pl
from jax.experimental.pallas import tpu as pltpu
from jax.sharding import PartitionSpec as P

MESH = pl.DeviceIdType.MESH
F32, BF16, I32 = jnp.float32, jnp.bfloat16, jnp.int32
HEADS, D = 12, 128
SEQ, SHOTS = 16, 16
ROWS = 128
OWN = SEQ * ROWS
CROSS = SHOTS * SEQ
KEYS = OWN + CROSS
QB = 256
KC = 768
SCALE = 1.0 / math.sqrt(D)
LOGIT2 = SCALE * math.log2(math.e)
MASKED = -1e30


def nt(a, b):
    return lax.dot_general(a, b, (((1,), (1,)), ((), ())), preferred_element_type=F32)


def nn(a, b):
    return jnp.dot(a, b, preferred_element_type=F32)


def zstep(i):
    return ((i + 1) // 2) * (2 * (i % 2) - 1)


def owns(t):
    r = t % 8
    return jnp.logical_or(r == 0, r % 3 != 0)


def head_of(t):
    r = t % 8
    return 6 * (t // 8) + r - (r + 4) // 8 - (r + 1) // 8


def at128(i):
    return pl.ds(pl.multiple_of(i * 128, 128), 128)


def at256(i):
    return pl.ds(pl.multiple_of(i * 256, 256), 256)


def attend(i, kx, vx, kb, qx, gx, kt, vt, logit, prob, dlog, gn, ox, dqx):
    rows = at256(i)
    q = qx[rows, :]
    g = gx[rows, :]
    qa = jnp.concatenate([q, jnp.ones((QB, D), BF16)], 1)
    top = None
    for c in range(KEYS // KC):
        ks = slice(c * KC, (c + 1) * KC)
        s = nt(jnp.concatenate([kx[ks, :], kb[ks, :]], 1), qa)
        logit[ks, :] = s
        m = jnp.max(s.reshape(KC // 8, 8, QB), axis=0)
        top = m if top is None else jnp.maximum(top, m)
    top = jnp.max(top, axis=0, keepdims=True) * LOGIT2
    acc = None
    for c in range(KEYS // KC):
        ks = slice(c * KC, (c + 1) * KC)
        p = jnp.exp2(logit[ks, :] * LOGIT2 - top).astype(BF16)
        prob[ks, rows] = p
        part = nn(vt[:, ks], p)
        acc = part if acc is None else acc + part
    total = jnp.broadcast_to(acc[128:129, :], (D, QB))
    both = jnp.concatenate([acc[:128], total], 0).T
    inv = 1.0 / both[:, 128:]
    att = (both[:, :128] * inv).astype(BF16)
    ox[rows, :] = att
    gf = g.astype(F32)
    delta = jnp.sum(gf * att.astype(F32), axis=1, keepdims=True) * inv
    gs = (gf * inv).astype(BF16)
    gn[rows, :] = gs
    high = delta.astype(BF16).astype(F32)
    lane = lax.broadcasted_iota(I32, (QB, D), 1)
    tail = jnp.where(lane == 0, high, jnp.where(lane == 1, delta - high, 0.0))
    ga = jnp.concatenate([gs, tail.astype(BF16)], 1)
    lane = lax.broadcasted_iota(I32, (KC, D), 1)
    minus = jnp.where(lane < 2, -1.0, 0.0).astype(BF16)
    acc = None
    for c in range(KEYS // KC):
        ks = slice(c * KC, (c + 1) * KC)
        dp = nt(jnp.concatenate([vx[ks, :], minus], 1), ga)
        ds = prob[ks, rows] * dp.astype(BF16)
        dlog[ks, rows] = ds
        part = nn(kt[:, ks], ds)
        acc = part if acc is None else acc + part
    dqx[rows, :] = (acc * SCALE).T.astype(BF16)


def kernel(
    lens, pos, q, k, v, g, o, dq, dk, dv,
    kx, vx, kb, qx, gx, kt, vt, logit, prob, dlog, gn, ox, dqx, dkx, dvx,
    xs, xg, xr, xc, xl, lk, lv,
    in_send, kv_recv, q_recv, g_recv, in_own, x_send, x_recv, out_send, out_recv, out_own, c_send, c_recv,
):
    me, sh = lax.axis_index("seq"), lax.axis_index("shot")
    z, x = me // 2, me % 2
    mine = owns(me)
    head = head_of(me)

    barrier = pltpu.get_barrier_semaphore()

    def greet(j, _):
        pl.semaphore_signal(barrier, inc=1, device_id=(sh, (me + j) % SEQ), device_id_type=MESH)
        pl.semaphore_signal(barrier, inc=1, device_id=((sh + j) % SHOTS, me), device_id_type=MESH)
        return 0

    lax.fori_loop(1, 16, greet, 0)
    pl.semaphore_wait(barrier, 30)

    def remote(src, dst, send, recv, to):
        return pltpu.make_async_remote_copy(
            src_ref=src, dst_ref=dst, send_sem=send, recv_sem=recv, device_id=to, device_id_type=MESH
        )

    def partner(j):
        return 2 * ((z - zstep(j // 2) + 8) % 8) + (x + j) % 2

    def send_kv(j, _):
        t = partner(j)

        @pl.when(owns(t))
        def _():
            cols = at128(head_of(t))
            remote(k.at[0, :, cols], kx.at[at128(me), :], in_send.at[0], kv_recv.at[0], (sh, t)).start()
            remote(v.at[0, :, cols], vx.at[at128(me), :], in_send.at[1], kv_recv.at[1], (sh, t)).start()

        return 0

    def send_qg(j, _):
        t = partner(j)
        i = j // 2

        @pl.when(owns(t))
        def _():
            cols = at128(head_of(t))
            slot = at128(2 * i + x)
            remote(q.at[0, :, cols], qx.at[slot, :], in_send.at[2], q_recv.at[i], (sh, t)).start()
            remote(g.at[0, :, cols], gx.at[slot, :], in_send.at[3], g_recv.at[i], (sh, t)).start()

        return 0

    def own_in():
        cols = at128(head)
        return (
            pltpu.make_async_copy(k.at[0, :, cols], kx.at[at128(me), :], in_own.at[0]),
            pltpu.make_async_copy(v.at[0, :, cols], vx.at[at128(me), :], in_own.at[1]),
            pltpu.make_async_copy(q.at[0, :, cols], qx.at[at128(x), :], in_own.at[2]),
            pltpu.make_async_copy(g.at[0, :, cols], gx.at[at128(x), :], in_own.at[3]),
        )

    def own_out():
        cols = at128(head)
        return (
            pltpu.make_async_copy(ox.at[at128(x), :], o.at[0, :, cols], out_own.at[0]),
            pltpu.make_async_copy(dqx.at[at128(x), :], dq.at[0, :, cols], out_own.at[1]),
            pltpu.make_async_copy(dkx.at[at128(me), :], lk.at[:, cols], out_own.at[2]),
            pltpu.make_async_copy(dvx.at[at128(me), :], lv.at[:, cols], out_own.at[3]),
        )

    @pl.when(mine)
    def _():
        for copy in own_in():
            copy.start()

    lax.fori_loop(1, SEQ, send_kv, 0)
    lax.fori_loop(1, SEQ, send_qg, 0)

    @pl.when(mine)
    def _():
        length = lens[sh]
        here = (sh, me)
        row = lax.broadcasted_iota(I32, (ROWS, D), 0)
        lane = lax.broadcasted_iota(I32, (ROWS, D), 1)
        for b in range(SEQ):
            alive = jnp.logical_or(row + b * ROWS < length, row + b * ROWS == pos[0, b])
            dead = jnp.logical_and(jnp.logical_not(alive), lane == 0)
            kb[b * ROWS : (b + 1) * ROWS, :] = jnp.where(dead, MASKED, 0.0).astype(BF16)
        for b in range(CROSS // ROWS):
            dead = jnp.logical_and((row + b * ROWS) // SEQ == sh, lane == 0)
            kb[OWN + b * ROWS : OWN + (b + 1) * ROWS, :] = jnp.where(dead, MASKED, 0.0).astype(BF16)
        vt[D : D + 16, :] = jnp.ones((16, KEYS), BF16)
        sub = lax.broadcasted_iota(I32, (SEQ, OWN), 0)
        at = jnp.full((SEQ, OWN), -1, I32)
        for b in range(SEQ):
            at = jnp.where(sub == b, pos[0, b], at)
        pick = jnp.where(lax.broadcasted_iota(I32, (SEQ, OWN), 1) == at, 1.0, 0.0).astype(BF16)

        for n, (buf, copy) in enumerate(zip((kx, vx), own_in())):
            part = buf.at[pl.ds(0, OWN - ROWS), :]
            remote(part, part, in_send.at[n], kv_recv.at[n], here).wait_recv()
            copy.wait()
            rows = nn(pick, buf[0:OWN, :]).astype(BF16)
            xs[n] = rows
            buf[pl.ds(pl.multiple_of(OWN + sh * SEQ, SEQ), SEQ), :] = rows

        def send_x(j, _):
            to = ((sh + j) % SHOTS, me)
            dst = pl.ds(pl.multiple_of(OWN + sh * SEQ, SEQ), SEQ)
            remote(xs.at[0], kx.at[dst, :], x_send.at[0], x_recv.at[0], to).start()
            remote(xs.at[1], vx.at[dst, :], x_send.at[1], x_recv.at[1], to).start()
            return 0

        lax.fori_loop(1, SHOTS, send_x, 0)

        def turn(c, _):
            kt[:, at256(c)] = kx[at256(c), :].T
            vt[0:D, at256(c)] = vx[at256(c), :].T
            return 0

        lax.fori_loop(0, OWN // 256, turn, 0)
        for n, buf in enumerate((kx, vx)):
            part = buf.at[pl.ds(OWN, CROSS - SEQ), :]
            remote(part, part, x_send.at[n], x_recv.at[n], here).wait()
        lax.fori_loop(OWN // 256, KEYS // 256, turn, 0)

        def step(i, _):
            for n, (buf, sem) in enumerate(((qx, q_recv), (gx, g_recv))):

                @pl.when(i == 0)
                def _(n=n, buf=buf, sem=sem):
                    part = buf.at[at128(1 - x), :]
                    remote(part, part, in_send.at[2 + n], sem.at[i], here).wait_recv()
                    own_in()[2 + n].wait()

                @pl.when(i > 0)
                def _(n=n, buf=buf, sem=sem):
                    part = buf.at[at256(i), :]
                    remote(part, part, in_send.at[2 + n], sem.at[i], here).wait_recv()

            attend(i, kx, vx, kb, qx, gx, kt, vt, logit, prob, dlog, gn, ox, dqx)
            cols = at128(head)
            for d in range(2):
                xt = (x + d) % 2
                to = (sh, 2 * ((z + zstep(i) + 8) % 8) + xt)
                slot = at128(2 * i + xt)

                def start(slot=slot, to=to):
                    remote(ox.at[slot, :], o.at[0, :, cols], out_send.at[0], out_recv.at[0], to).start()
                    remote(dqx.at[slot, :], dq.at[0, :, cols], out_send.at[1], out_recv.at[1], to).start()

                if d == 1:
                    start()
                else:
                    pl.when(i > 0)(start)

                    @pl.when(i == 0)
                    def _():
                        own_out()[0].start()
                        own_out()[1].start()

            return 0

        lax.fori_loop(0, SEQ // 2, step, 0)

        cross = pl.ds(OWN, CROSS)
        xg[:, 0:SEQ, :] = (nn(dlog[cross, :], qx[...]) * SCALE).reshape(SHOTS, SEQ, D)
        xg[:, SEQ : 2 * SEQ, :] = nn(prob[cross, :], gn[...]).reshape(SHOTS, SEQ, D)
        xr[pl.ds(sh, 1)] = jnp.zeros((1, 2 * SEQ, D), F32)

        def send_g(j, _):
            s = (sh + j) % SHOTS
            remote(xg.at[s], xr.at[sh], x_send.at[2], x_recv.at[2], (s, me)).start()
            return 0

        lax.fori_loop(1, SHOTS, send_g, 0)

        def finish(i, _):
            zt = (z + zstep(i) + 8) % 8
            rows = at256(zt)
            cols = at128(head)
            dkx[rows, :] = (nn(dlog[rows, :], qx[...]) * SCALE).astype(BF16)
            dvx[rows, :] = nn(prob[rows, :], gn[...]).astype(BF16)
            for d in range(2):
                t = 2 * zt + (x + d) % 2

                def start(t=t):
                    remote(dkx.at[at128(t), :], lk.at[:, cols], out_send.at[2], out_recv.at[2], (sh, t)).start()
                    remote(dvx.at[at128(t), :], lv.at[:, cols], out_send.at[3], out_recv.at[3], (sh, t)).start()

                if d == 1:
                    start()
                else:
                    pl.when(i > 0)(start)

                    @pl.when(i == 0)
                    def _():
                        own_out()[2].start()
                        own_out()[3].start()

            return 0

        lax.fori_loop(0, SEQ // 2, finish, 0)

        part = xr.at[pl.ds(0, SHOTS - 1)]
        remote(part, part, x_send.at[2], x_recv.at[2], here).wait()
        total = jnp.sum(xr[...], axis=0)
        xc[...] = jnp.zeros_like(xc)
        for b in range(SEQ):
            xc[b, 0:1, :] = total[b : b + 1, :]
            xc[b, 1:2, :] = total[SEQ + b : SEQ + b + 1, :]
        xl[pl.ds(head, 1)] = xc[pl.ds(me, 1)]

        def send_c(j, _):
            t = (me + j) % SEQ
            remote(xc.at[t], xl.at[head], c_send, c_recv, (sh, t)).start()
            return 0

        lax.fori_loop(1, SEQ, send_c, 0)

        for n, buf in enumerate((ox, dqx, dkx, dvx)):
            part = buf.at[pl.ds(0, OWN - ROWS), :]
            remote(part, part, out_send.at[n], out_recv.at[n], here).wait_send()
            own_out()[n].wait()
        part = xc.at[pl.ds(0, SEQ - 1)]
        remote(part, part, c_send, c_recv, here).wait_send()

    def settle(count):
        here = (sh, me)
        for n, buf in enumerate((k, v, q, g)):
            part = buf.at[0, :, pl.ds(0, count * D)]
            remote(part, part, in_send.at[n], out_recv.at[n], here).wait_send()
        for n, buf in enumerate((o.at[0], dq.at[0], lk, lv)):
            part = buf.at[:, pl.ds(0, count * D)]
            remote(part, part, out_send.at[n], out_recv.at[n], here).wait_recv()
        part = xl.at[pl.ds(0, count)]
        remote(part, part, c_send, c_recv, here).wait_recv()

    @pl.when(mine)
    def _():
        settle(HEADS - 1)

    @pl.when(jnp.logical_not(mine))
    def _():
        settle(HEADS)

    there = lax.broadcasted_iota(I32, (ROWS, D), 0) == pos[0, me] - me * ROWS
    for h in range(HEADS):
        cols = slice(h * D, (h + 1) * D)
        add = xl[h]
        dk[0, :, cols] = (lk[:, cols].astype(F32) + jnp.where(there, add[0:1, :], 0.0)).astype(BF16)
        dv[0, :, cols] = (lv[:, cols].astype(F32) + jnp.where(there, add[1:2, :], 0.0)).astype(BF16)


def body(query_rows, key_rows, value_rows, out_grad, shot_lengths, global_positions):
    smem = pl.BlockSpec(memory_space=pltpu.SMEM)
    hbm = pl.BlockSpec(memory_space=pl.ANY)
    vmem = pl.BlockSpec(memory_space=pltpu.VMEM)
    shape = jax.ShapeDtypeStruct(query_rows.shape, BF16)
    dma = pltpu.SemaphoreType.DMA
    return tuple(
        pl.pallas_call(
            kernel,
            out_shape=(shape,) * 4,
            in_specs=[smem, smem, hbm, hbm, hbm, hbm],
            out_specs=(hbm, hbm, vmem, vmem),
            scratch_shapes=[
                pltpu.VMEM((KEYS, D), BF16),
                pltpu.VMEM((KEYS, D), BF16),
                pltpu.VMEM((KEYS, D), BF16),
                pltpu.VMEM((OWN, D), BF16),
                pltpu.VMEM((OWN, D), BF16),
                pltpu.VMEM((D, KEYS), BF16),
                pltpu.VMEM((D + 16, KEYS), BF16),
                pltpu.VMEM((KEYS, QB), F32),
                pltpu.VMEM((KEYS, OWN), BF16),
                pltpu.VMEM((KEYS, OWN), BF16),
                pltpu.VMEM((OWN, D), BF16),
                pltpu.VMEM((OWN, D), BF16),
                pltpu.VMEM((OWN, D), BF16),
                pltpu.VMEM((OWN, D), BF16),
                pltpu.VMEM((OWN, D), BF16),
                pltpu.VMEM((2, SEQ, D), BF16),
                pltpu.VMEM((SHOTS, 2 * SEQ, D), F32),
                pltpu.VMEM((SHOTS, 2 * SEQ, D), F32),
                pltpu.VMEM((SEQ, 8, D), F32),
                pltpu.VMEM((HEADS, 8, D), F32),
                pltpu.VMEM((ROWS, HEADS * D), BF16),
                pltpu.VMEM((ROWS, HEADS * D), BF16),
                dma((4,)),
                dma((2,)),
                dma((SEQ // 2,)),
                dma((SEQ // 2,)),
                dma((4,)),
                dma((3,)),
                dma((3,)),
                dma((4,)),
                dma((4,)),
                dma((4,)),
                dma,
                dma,
            ],
            compiler_params=pltpu.CompilerParams(
                collective_id=0, has_side_effects=True, vmem_limit_bytes=48 << 20
            ),
        )(shot_lengths, global_positions, query_rows, key_rows, value_rows, out_grad)
    )


def solution(mesh):
    rows = P("shot", "seq", None)
    return jax.shard_map(
        body,
        mesh=mesh,
        in_specs=(rows, rows, rows, rows, P(), P("shot", None)),
        out_specs=(rows,) * 4,
        check_vma=False,
    )
```

```python
import math

import jax
import jax.numpy as jnp
from jax import lax
from jax.experimental import pallas as pl
from jax.experimental.pallas import tpu as pltpu
from jax.sharding import PartitionSpec as P

MESH = pl.DeviceIdType.MESH
F32, BF16, I32 = jnp.float32, jnp.bfloat16, jnp.int32
HEADS, D = 12, 128
SEQ, SHOTS = 16, 16
ROWS = 128
OWN = SEQ * ROWS
CROSS = SHOTS * SEQ
KEYS = OWN + CROSS
QB = 256
KC = 768
SCALE = 1.0 / math.sqrt(D)
LOGIT2 = SCALE * math.log2(math.e)
MASKED = -1e30
EARLY = 5
CLOSE = 4
IDLE = ((0, 2, 5, 7), (8, 10, 13, 15))


def nt(a, b):
    return lax.dot_general(a, b, (((1,), (1,)), ((), ())), preferred_element_type=F32)


def nn(a, b):
    return jnp.dot(a, b, preferred_element_type=F32)


def zstep(i):
    return ((i + 1) // 2) * (2 * (i % 2) - 1)


def idle(shot):
    core = shot % 2
    return tuple(a + core * (b - a) for a, b in zip(*IDLE))


def owns(t, shot):
    found = t >= 0
    for s in idle(shot):
        found = jnp.logical_and(found, t != s)
    return found


def head_of(t, shot):
    return t - sum((t - s + 15) // 16 for s in idle(shot))


def owner_of(h, shot):
    return h + sum((h + n - s + 16) // 16 for n, s in enumerate(idle(shot)))


def at128(i):
    return pl.ds(pl.multiple_of(i * 128, 128), 128)


def at256(i):
    return pl.ds(pl.multiple_of(i * 256, 256), 256)


def attend(i, kx, vx, kb, qx, gx, kt, vt, logit, prob, dlog, gn, ox, dqx):
    rows = at256(i)
    q = qx[rows, :]
    g = gx[rows, :]
    qa = jnp.concatenate([q, jnp.ones((QB, D), BF16)], 1)
    top = None
    for c in range(KEYS // KC):
        ks = slice(c * KC, (c + 1) * KC)
        s = nt(jnp.concatenate([kx[ks, :], kb[ks, :]], 1), qa)
        logit[ks, :] = s
        m = jnp.max(s.reshape(KC // 8, 8, QB), axis=0)
        top = m if top is None else jnp.maximum(top, m)
    top = jnp.max(top, axis=0, keepdims=True) * LOGIT2
    acc = None
    for c in range(KEYS // KC):
        ks = slice(c * KC, (c + 1) * KC)
        p = jnp.exp2(logit[ks, :] * LOGIT2 - top).astype(BF16)
        prob[ks, rows] = p
        part = nn(vt[:, ks], p)
        acc = part if acc is None else acc + part
    total = jnp.broadcast_to(acc[128:129, :], (D, QB))
    both = jnp.concatenate([acc[:128], total], 0).T
    inv = 1.0 / both[:, 128:]
    att = (both[:, :128] * inv).astype(BF16)
    ox[rows, :] = att
    gf = g.astype(F32)
    delta = jnp.sum(gf * att.astype(F32), axis=1, keepdims=True) * inv
    gs = (gf * inv).astype(BF16)
    gn[rows, :] = gs
    high = delta.astype(BF16).astype(F32)
    lane = lax.broadcasted_iota(I32, (QB, D), 1)
    tail = jnp.where(lane == 0, high, jnp.where(lane == 1, delta - high, 0.0))
    ga = jnp.concatenate([gs, tail.astype(BF16)], 1)
    lane = lax.broadcasted_iota(I32, (KC, D), 1)
    minus = jnp.where(lane < 2, -1.0, 0.0).astype(BF16)
    acc = None
    for c in range(KEYS // KC):
        ks = slice(c * KC, (c + 1) * KC)
        dp = nt(jnp.concatenate([vx[ks, :], minus], 1), ga)
        ds = prob[ks, rows] * dp.astype(BF16)
        dlog[ks, rows] = ds
        part = nn(kt[:, ks], ds)
        acc = part if acc is None else acc + part
    dqx[rows, :] = (acc * SCALE).T.astype(BF16)


def kernel(
    lens_hbm, pos_hbm, q, k, v, g, o, dq, lk, lv, xl, lens, pos,
    kx, vx, kb, qx, gx, kt, vt, logit, prob, dlog, gn, ox, dqx, dkx, dvx,
    kin, vin, rowt, xin, xs, xg, xr, xc,
    in_send, kv_recv, q_recv, g_recv, in_own, x_send, x_recv, out_send, out_recv, out_own, c_send, c_recv, s_own, r_send, r_recv,
):
    me, sh = lax.axis_index("seq"), lax.axis_index("shot")
    z, x = me // 2, me % 2
    mine = owns(me, sh)
    head = head_of(me, sh)

    scalars = [
        pltpu.make_async_copy(lens_hbm, lens, s_own.at[0]),
        pltpu.make_async_copy(pos_hbm, pos, s_own.at[1]),
    ]
    whole = [
        pltpu.make_async_copy(k.at[0], kin, s_own.at[2]),
        pltpu.make_async_copy(v.at[0], vin, s_own.at[3]),
    ]
    for copy in scalars + whole:
        copy.start()
    barrier = pltpu.get_barrier_semaphore()

    def greet(j, _):
        pl.semaphore_signal(barrier, inc=1, device_id=(sh, (me + j) % SEQ), device_id_type=MESH)
        return 0

    def sibling(j):
        s = (sh + j) % SHOTS
        return (s, owner_of(head, s))

    def greet_sibling(j, _):
        pl.semaphore_signal(barrier, inc=1, device_id=sibling(j), device_id_type=MESH)
        return 0

    lax.fori_loop(1, SEQ, greet, 0)

    @pl.when(mine)
    def _():
        lax.fori_loop(1, SHOTS, greet_sibling, 0)

    for copy in scalars + whole:
        copy.wait()
    chosen = lax.broadcasted_iota(I32, (8, ROWS), 1) == pos[0, me] - me * ROWS
    sub = lax.broadcasted_iota(I32, (8, ROWS), 0)
    first = jnp.where(jnp.logical_and(chosen, sub == 0), 1.0, 0.0).astype(BF16)
    second = jnp.where(jnp.logical_and(chosen, sub == 1), 1.0, 0.0).astype(BF16)
    rowt[...] = nn(first, kin[...]) + nn(second, vin[...])

    @pl.when(mine)
    def _():
        pl.semaphore_wait(barrier, SEQ + SHOTS - 2)

    @pl.when(jnp.logical_not(mine))
    def _():
        pl.semaphore_wait(barrier, SEQ - 1)

    def remote(src, dst, send, recv, to):
        return pltpu.make_async_remote_copy(
            src_ref=src, dst_ref=dst, send_sem=send, recv_sem=recv, device_id=to, device_id_type=MESH
        )

    def partner(j):
        return 2 * ((z - zstep(j // 2) + 8) % 8) + (x + j) % 2

    def send_row(j, _):
        t = partner(j)

        @pl.when(owns(t, sh))
        def _():
            cols = at128(head_of(t, sh))
            remote(rowt.at[:, cols], xin.at[me], r_send, r_recv, (sh, t)).start()

        return 0

    def own_row():
        return pltpu.make_async_copy(rowt.at[:, at128(head)], xin.at[me], in_own.at[4])

    def send_kv(j, _):
        t = partner(j)

        @pl.when(owns(t, sh))
        def _():
            cols = at128(head_of(t, sh))
            remote(k.at[0, :, cols], kx.at[at128(me), :], in_send.at[0], kv_recv.at[0], (sh, t)).start()
            remote(v.at[0, :, cols], vx.at[at128(me), :], in_send.at[1], kv_recv.at[1], (sh, t)).start()

        return 0

    def send_qg(j, _):
        t = partner(j)
        i = j // 2

        @pl.when(owns(t, sh))
        def _():
            cols = at128(head_of(t, sh))
            slot = at128(2 * i + x)
            remote(q.at[0, :, cols], qx.at[slot, :], in_send.at[2], q_recv.at[i], (sh, t)).start()
            remote(g.at[0, :, cols], gx.at[slot, :], in_send.at[3], g_recv.at[i], (sh, t)).start()

        return 0

    def own_in(n):
        cols = at128(head)
        src = (k, v, q, g)[n].at[0, :, cols]
        dst = (kx, vx, qx, gx)[n].at[at128(me if n < 2 else x), :]
        return pltpu.make_async_copy(src, dst, in_own.at[n])

    def own_out(n):
        cols = at128(head)
        src = (ox, dqx, dkx, dvx)[n].at[at128(x if n < 2 else me), :]
        dst = (o, dq, lk, lv)[n].at[0, :, cols]
        return pltpu.make_async_copy(src, dst, out_own.at[n])

    def own_c():
        return pltpu.make_async_copy(xc.at[me], xl.at[head], out_own.at[4])

    @pl.when(mine)
    def _():
        for n in range(4):
            own_in(n).start()
        own_row().start()

    lax.fori_loop(1, SEQ, send_row, 0)
    lax.fori_loop(1, EARLY, send_kv, 0)

    @pl.when(mine)
    def _():
        remote(xin.at[pl.ds(0, SEQ - 1)], xin.at[pl.ds(0, SEQ - 1)], r_send, r_recv, (sh, me)).wait_recv()
        own_row().wait()
        dst = pl.ds(pl.multiple_of(OWN + sh * SEQ, SEQ), SEQ)
        for n, buf in enumerate((kx, vx)):
            rows = xin[:, n, :].astype(BF16)
            xs[n] = rows
            buf[dst, :] = rows

        def send_x(j, _):
            to = sibling(j)
            remote(xs.at[0], kx.at[dst, :], x_send.at[0], x_recv.at[0], to).start()
            remote(xs.at[1], vx.at[dst, :], x_send.at[1], x_recv.at[1], to).start()
            return 0

        lax.fori_loop(1, SHOTS, send_x, 0)

    lax.fori_loop(EARLY, SEQ, send_kv, 0)
    lax.fori_loop(1, SEQ, send_qg, 0)

    @pl.when(mine)
    def _():
        length = lens[sh]
        here = (sh, me)
        row = lax.broadcasted_iota(I32, (ROWS, D), 0)
        lane = lax.broadcasted_iota(I32, (ROWS, D), 1)
        for b in range(SEQ):
            alive = jnp.logical_or(row + b * ROWS < length, row + b * ROWS == pos[0, b])
            dead = jnp.logical_and(jnp.logical_not(alive), lane == 0)
            kb[b * ROWS : (b + 1) * ROWS, :] = jnp.where(dead, MASKED, 0.0).astype(BF16)
        for b in range(CROSS // ROWS):
            dead = jnp.logical_and((row + b * ROWS) // SEQ == sh, lane == 0)
            kb[OWN + b * ROWS : OWN + (b + 1) * ROWS, :] = jnp.where(dead, MASKED, 0.0).astype(BF16)
        vt[D : D + 16, :] = jnp.ones((16, KEYS), BF16)
        for n, buf in enumerate((kx, vx)):
            part = buf.at[pl.ds(0, OWN - ROWS), :]
            remote(part, part, in_send.at[n], kv_recv.at[n], here).wait_recv()
            own_in(n).wait()

        def turn(c, _):
            kt[:, at256(c)] = kx[at256(c), :].T
            vt[0:D, at256(c)] = vx[at256(c), :].T
            return 0

        lax.fori_loop(0, OWN // 256, turn, 0)
        for n, buf in enumerate((kx, vx)):
            part = buf.at[pl.ds(OWN, CROSS - SEQ), :]
            remote(part, part, x_send.at[n], x_recv.at[n], here).wait()
        lax.fori_loop(OWN // 256, KEYS // 256, turn, 0)

        def step(i, _):
            for n, (buf, sem) in enumerate(((qx, q_recv), (gx, g_recv))):

                @pl.when(i == 0)
                def _(n=n, buf=buf, sem=sem):
                    part = buf.at[at128(1 - x), :]
                    remote(part, part, in_send.at[2 + n], sem.at[i], here).wait_recv()
                    own_in(2 + n).wait()

                @pl.when(i > 0)
                def _(n=n, buf=buf, sem=sem):
                    part = buf.at[at256(i), :]
                    remote(part, part, in_send.at[2 + n], sem.at[i], here).wait_recv()

            attend(i, kx, vx, kb, qx, gx, kt, vt, logit, prob, dlog, gn, ox, dqx)
            cols = at128(head)
            for d in range(2):
                xt = (x + d) % 2
                to = (sh, 2 * ((z + zstep(i) + 8) % 8) + xt)
                slot = at128(2 * i + xt)

                def start(slot=slot, to=to):
                    remote(ox.at[slot, :], o.at[0, :, cols], out_send.at[0], out_recv.at[0], to).start()
                    remote(dqx.at[slot, :], dq.at[0, :, cols], out_send.at[1], out_recv.at[1], to).start()

                if d == 1:
                    start()
                else:
                    pl.when(i > 0)(start)

                    @pl.when(i == 0)
                    def _():
                        own_out(0).start()
                        own_out(1).start()

            return 0

        lax.fori_loop(0, SEQ // 2, step, 0)

        cross = pl.ds(OWN, CROSS)
        xg[:, 0:SEQ, :] = (nn(dlog[cross, :], qx[...]) * SCALE).reshape(SHOTS, SEQ, D)
        xg[:, SEQ : 2 * SEQ, :] = nn(prob[cross, :], gn[...]).reshape(SHOTS, SEQ, D)
        xr[pl.ds(sh, 1)] = jnp.zeros((1, 2 * SEQ, D), F32)

        def send_g(j, _):
            s = (sh + j) % SHOTS
            remote(xg.at[s], xr.at[sh], x_send.at[2], x_recv.at[2], sibling(j)).start()
            return 0

        lax.fori_loop(1, SHOTS, send_g, 0)

        def send_c(j, _):
            t = (me + j) % SEQ
            remote(xc.at[t], xl.at[head], c_send, c_recv, (sh, t)).start()
            return 0

        def close():
            part = xr.at[pl.ds(0, SHOTS - 1)]
            remote(part, part, x_send.at[2], x_recv.at[2], here).wait()
            total = jnp.sum(xr[...], axis=0)
            xc[...] = jnp.zeros_like(xc)
            for b in range(SEQ):
                xc[b, 0:1, :] = total[b : b + 1, :]
                xc[b, 1:2, :] = total[SEQ + b : SEQ + b + 1, :]
            own_c().start()
            lax.fori_loop(1, SEQ, send_c, 0)

        def finish(i, _):
            pl.when(i == CLOSE)(close)
            zt = (z + zstep(i) + 8) % 8
            rows = at256(zt)
            cols = at128(head)
            dkx[rows, :] = (nn(dlog[rows, :], qx[...]) * SCALE).astype(BF16)
            dvx[rows, :] = nn(prob[rows, :], gn[...]).astype(BF16)
            for d in range(2):
                t = 2 * zt + (x + d) % 2

                def start(t=t):
                    remote(dkx.at[at128(t), :], lk.at[0, :, cols], out_send.at[2], out_recv.at[2], (sh, t)).start()
                    remote(dvx.at[at128(t), :], lv.at[0, :, cols], out_send.at[3], out_recv.at[3], (sh, t)).start()

                if d == 1:
                    start()
                else:
                    pl.when(i > 0)(start)

                    @pl.when(i == 0)
                    def _():
                        own_out(2).start()
                        own_out(3).start()

            return 0

        lax.fori_loop(0, SEQ // 2, finish, 0)

        for n, buf in enumerate((ox, dqx, dkx, dvx)):
            part = buf.at[pl.ds(0, OWN - ROWS), :]
            remote(part, part, out_send.at[n], out_recv.at[n], here).wait_send()
            own_out(n).wait()
        own_c().wait()
        part = xc.at[pl.ds(0, SEQ - 1)]
        remote(part, part, c_send, c_recv, here).wait_send()

    def settle(count):
        here = (sh, me)
        part = xl.at[pl.ds(0, count)]
        remote(part, part, c_send, c_recv, here).wait_recv()
        for n, buf in enumerate((o, dq, lk, lv)):
            part = buf.at[0, :, pl.ds(0, count * D)]
            remote(part, part, out_send.at[n], out_recv.at[n], here).wait_recv()
        part = rowt.at[:, pl.ds(0, count * D)]
        remote(part, part, r_send, r_recv, here).wait_send()
        for n, buf in enumerate((k, v, q, g)):
            part = buf.at[0, :, pl.ds(0, count * D)]
            remote(part, part, in_send.at[n], out_recv.at[n], here).wait_send()

    @pl.when(mine)
    def _():
        settle(HEADS - 1)

    @pl.when(jnp.logical_not(mine))
    def _():
        settle(HEADS)


def hand_over(pos_hbm, o, dq, lk, lv, xl_hbm, o_out, dq_out, dk_out, dv_out, pos, xl, bufs, come, go):
    small = [
        pltpu.make_async_copy(pos_hbm, pos, come.at[4]),
        pltpu.make_async_copy(xl_hbm, xl, come.at[5]),
    ]
    into = [pltpu.make_async_copy(ref, bufs.at[n], come.at[n]) for n, ref in enumerate((lk, lv, o, dq))]
    out = [pltpu.make_async_copy(bufs.at[n], ref, go.at[n]) for n, ref in enumerate((dk_out, dv_out, o_out, dq_out))]
    for copy in small + into:
        copy.start()
    for copy in small:
        copy.wait()
    me = lax.axis_index("seq")
    there = lax.broadcasted_iota(I32, (ROWS, D), 0) == pos[0, me] - me * ROWS
    for n in range(4):
        into[n].wait()
        if n < 2:
            for h in range(HEADS):
                cols = slice(h * D, (h + 1) * D)
                add = jnp.where(there, xl[h][n : n + 1, :], 0.0)
                bufs[n, 0, :, cols] = (bufs[n, 0, :, cols].astype(F32) + add).astype(BF16)
        out[n].start()
    for copy in out:
        copy.wait()


def body(query_rows, key_rows, value_rows, out_grad, shot_lengths, global_positions):
    hbm = pl.BlockSpec(memory_space=pltpu.HBM)
    shape = jax.ShapeDtypeStruct(query_rows.shape, BF16)
    dma = pltpu.SemaphoreType.DMA
    results = pl.pallas_call(
        kernel,
        out_shape=(shape,) * 4 + (jax.ShapeDtypeStruct((HEADS, 8, D), F32),),
        in_specs=[hbm] * 6,
        out_specs=(hbm,) * 5,
        scratch_shapes=[
            pltpu.SMEM((SHOTS,), I32),
            pltpu.SMEM((1, SEQ), I32),
            pltpu.VMEM((KEYS, D), BF16),
            pltpu.VMEM((KEYS, D), BF16),
            pltpu.VMEM((KEYS, D), BF16),
            pltpu.VMEM((OWN, D), BF16),
            pltpu.VMEM((OWN, D), BF16),
            pltpu.VMEM((D, KEYS), BF16),
            pltpu.VMEM((D + 16, KEYS), BF16),
            pltpu.VMEM((KEYS, QB), F32),
            pltpu.VMEM((KEYS, OWN), BF16),
            pltpu.VMEM((KEYS, OWN), BF16),
            pltpu.VMEM((OWN, D), BF16),
            pltpu.VMEM((OWN, D), BF16),
            pltpu.VMEM((OWN, D), BF16),
            pltpu.VMEM((OWN, D), BF16),
            pltpu.VMEM((OWN, D), BF16),
            pltpu.VMEM((ROWS, HEADS * D), BF16),
            pltpu.VMEM((ROWS, HEADS * D), BF16),
            pltpu.VMEM((8, HEADS * D), F32),
            pltpu.VMEM((SEQ, 8, D), F32),
            pltpu.VMEM((2, SEQ, D), BF16),
            pltpu.VMEM((SHOTS, 2 * SEQ, D), F32),
            pltpu.VMEM((SHOTS, 2 * SEQ, D), F32),
            pltpu.VMEM((SEQ, 8, D), F32),
            dma((4,)),
            dma((2,)),
            dma((SEQ // 2,)),
            dma((SEQ // 2,)),
            dma((5,)),
            dma((3,)),
            dma((3,)),
            dma((4,)),
            dma((4,)),
            dma((5,)),
            dma,
            dma,
            dma((4,)),
            dma,
            dma,
        ],
        compiler_params=pltpu.CompilerParams(
            collective_id=0, has_side_effects=True, vmem_limit_bytes=63 << 20
        ),
    )(shot_lengths, global_positions, query_rows, key_rows, value_rows, out_grad)
    return pl.pallas_call(
        hand_over,
        out_shape=(shape,) * 4,
        in_specs=[hbm] * 6,
        out_specs=(hbm,) * 4,
        scratch_shapes=[
            pltpu.SMEM((1, SEQ), I32),
            pltpu.VMEM((HEADS, 8, D), F32),
            pltpu.VMEM((4, 1, ROWS, HEADS * D), BF16),
            dma((6,)),
            dma((4,)),
        ],
        compiler_params=pltpu.CompilerParams(vmem_limit_bytes=63 << 20),
    )(global_positions, *results)


def solution(mesh):
    rows = P("shot", "seq", None)
    return jax.shard_map(
        body,
        mesh=mesh,
        in_specs=(rows, rows, rows, rows, P(), P("shot", None)),
        out_specs=(rows,) * 4,
        check_vma=False,
    )
```

```python
import math

import jax
import jax.numpy as jnp
from jax import lax
from jax.experimental import pallas as pl
from jax.experimental.pallas import tpu as pltpu
from jax.sharding import PartitionSpec as P

MESH = pl.DeviceIdType.MESH
F32, BF16, I32 = jnp.float32, jnp.bfloat16, jnp.int32
HEADS, D = 12, 128
SEQ, SHOTS = 16, 16
ROWS = 128
OWN = SEQ * ROWS
CROSS = SHOTS * SEQ
KEYS = OWN + CROSS
QB = 256
KC = 768
SCALE = 1.0 / math.sqrt(D)
LOGIT2 = SCALE * math.log2(math.e)
MASKED = -1e30
CLOSE = 4
IDLE = ((1, 4, 10, 12), (2, 7, 9, 15))


def nt(a, b):
    return lax.dot_general(a, b, (((1,), (1,)), ((), ())), preferred_element_type=F32)


def nn(a, b):
    return jnp.dot(a, b, preferred_element_type=F32)


def zstep(i):
    return ((i + 1) // 2) * (2 * (i % 2) - 1)


def idle(shot):
    core = shot % 2
    return tuple(a + core * (b - a) for a, b in zip(*IDLE))


def owns(t, shot):
    found = t >= 0
    for s in idle(shot):
        found = jnp.logical_and(found, t != s)
    return found


def head_of(t, shot):
    return t - sum((t - s + 15) // 16 for s in idle(shot))


def owner_of(h, shot):
    return h + sum((h + n - s + 16) // 16 for n, s in enumerate(idle(shot)))


def at128(i):
    return pl.ds(pl.multiple_of(i * 128, 128), 128)


def at256(i):
    return pl.ds(pl.multiple_of(i * 256, 256), 256)


def attend(i, kx, vx, kb, qx, gx, kt, vt, logit, prob, dlog, gn, ox, dqx):
    rows = at256(i)
    q = qx[rows, :]
    g = gx[rows, :]
    qa = jnp.concatenate([q, jnp.ones((QB, D), BF16)], 1)
    top = None
    for c in range(KEYS // KC):
        ks = slice(c * KC, (c + 1) * KC)
        s = nt(jnp.concatenate([kx[ks, :], kb[ks, :]], 1), qa)
        logit[ks, :] = s
        m = jnp.max(s.reshape(KC // 8, 8, QB), axis=0)
        top = m if top is None else jnp.maximum(top, m)
    top = jnp.max(top, axis=0, keepdims=True) * LOGIT2
    acc = None
    for c in range(KEYS // KC):
        ks = slice(c * KC, (c + 1) * KC)
        p = jnp.exp2(logit[ks, :] * LOGIT2 - top).astype(BF16)
        prob[ks, rows] = p
        part = nn(vt[:, ks], p)
        acc = part if acc is None else acc + part
    total = jnp.broadcast_to(acc[128:129, :], (D, QB))
    both = jnp.concatenate([acc[:128], total], 0).T
    inv = 1.0 / both[:, 128:]
    att = (both[:, :128] * inv).astype(BF16)
    ox[rows, :] = att
    gf = g.astype(F32)
    delta = jnp.sum(gf * att.astype(F32), axis=1, keepdims=True) * inv
    gs = (gf * inv).astype(BF16)
    gn[rows, :] = gs
    high = delta.astype(BF16).astype(F32)
    lane = lax.broadcasted_iota(I32, (QB, D), 1)
    tail = jnp.where(lane == 0, high, jnp.where(lane == 1, delta - high, 0.0))
    ga = jnp.concatenate([gs, tail.astype(BF16)], 1)
    lane = lax.broadcasted_iota(I32, (KC, D), 1)
    minus = jnp.where(lane < 2, -1.0, 0.0).astype(BF16)
    acc = None
    for c in range(KEYS // KC):
        ks = slice(c * KC, (c + 1) * KC)
        dp = nt(jnp.concatenate([vx[ks, :], minus], 1), ga)
        ds = prob[ks, rows] * dp.astype(BF16)
        dlog[ks, rows] = ds
        part = nn(kt[:, ks], ds)
        acc = part if acc is None else acc + part
    dqx[rows, :] = (acc * SCALE).T.astype(BF16)


def kernel(
    lens_hbm, pos_hbm, q, k, v, g, o, dq, lk, lv, xl, lens, pos,
    kx, vx, kb, qx, gx, kt, vt, logit, prob, dlog, gn, ox, dqx, dkx, dvx,
    kin, vin, rowt, xin, xs, xg, xr, xc,
    in_send, kv_recv, q_recv, g_recv, in_own, x_send, x_recv, out_send, out_recv, out_own, c_send, c_recv, s_own, r_send, r_recv,
):
    me, sh = lax.axis_index("seq"), lax.axis_index("shot")
    z, x = me // 2, me % 2
    mine = owns(me, sh)
    head = head_of(me, sh)

    scalars = [
        pltpu.make_async_copy(lens_hbm, lens, s_own.at[0]),
        pltpu.make_async_copy(pos_hbm, pos, s_own.at[1]),
    ]
    whole = [
        pltpu.make_async_copy(k.at[0], kin, s_own.at[2]),
        pltpu.make_async_copy(v.at[0], vin, s_own.at[3]),
    ]
    for copy in scalars + whole:
        copy.start()
    barrier = pltpu.get_barrier_semaphore()

    def greet(j, _):
        pl.semaphore_signal(barrier, inc=1, device_id=(sh, (me + j) % SEQ), device_id_type=MESH)
        return 0

    def sibling(j):
        s = (sh + j) % SHOTS
        return (s, owner_of(head, s))

    def greet_sibling(j, _):
        pl.semaphore_signal(barrier, inc=1, device_id=sibling(j), device_id_type=MESH)
        return 0

    lax.fori_loop(1, SEQ, greet, 0)

    @pl.when(mine)
    def _():
        lax.fori_loop(1, SHOTS, greet_sibling, 0)

    for copy in scalars + whole:
        copy.wait()
    chosen = lax.broadcasted_iota(I32, (8, ROWS), 1) == pos[0, me] - me * ROWS
    sub = lax.broadcasted_iota(I32, (8, ROWS), 0)
    first = jnp.where(jnp.logical_and(chosen, sub == 0), 1.0, 0.0).astype(BF16)
    second = jnp.where(jnp.logical_and(chosen, sub == 1), 1.0, 0.0).astype(BF16)
    rowt[...] = nn(first, kin[...]) + nn(second, vin[...])

    @pl.when(mine)
    def _():
        pl.semaphore_wait(barrier, SEQ + SHOTS - 2)

    @pl.when(jnp.logical_not(mine))
    def _():
        pl.semaphore_wait(barrier, SEQ - 1)

    def remote(src, dst, send, recv, to):
        return pltpu.make_async_remote_copy(
            src_ref=src, dst_ref=dst, send_sem=send, recv_sem=recv, device_id=to, device_id_type=MESH
        )

    def partner(j):
        return 2 * ((z - zstep(j // 2) + 8) % 8) + (x + j) % 2

    def send_row(j, _):
        t = partner(j)

        @pl.when(owns(t, sh))
        def _():
            cols = at128(head_of(t, sh))
            remote(rowt.at[:, cols], xin.at[me], r_send, r_recv, (sh, t)).start()

        return 0

    def own_row():
        return pltpu.make_async_copy(rowt.at[:, at128(head)], xin.at[me], in_own.at[4])

    def send_kv(j, _):
        t = partner(j)

        @pl.when(owns(t, sh))
        def _():
            cols = at128(head_of(t, sh))
            remote(k.at[0, :, cols], kx.at[at128(me), :], in_send.at[0], kv_recv.at[0], (sh, t)).start()
            remote(v.at[0, :, cols], vx.at[at128(me), :], in_send.at[1], kv_recv.at[1], (sh, t)).start()

        return 0

    def send_qg(j, _):
        t = partner(j)
        i = j // 2

        @pl.when(owns(t, sh))
        def _():
            cols = at128(head_of(t, sh))
            slot = at128(2 * i + x)
            remote(q.at[0, :, cols], qx.at[slot, :], in_send.at[2], q_recv.at[i], (sh, t)).start()
            remote(g.at[0, :, cols], gx.at[slot, :], in_send.at[3], g_recv.at[i], (sh, t)).start()

        return 0

    def own_in(n):
        cols = at128(head)
        src = (k, v, q, g)[n].at[0, :, cols]
        dst = (kx, vx, qx, gx)[n].at[at128(me if n < 2 else x), :]
        return pltpu.make_async_copy(src, dst, in_own.at[n])

    def own_out(n):
        cols = at128(head)
        src = (ox, dqx, dkx, dvx)[n].at[at128(x if n < 2 else me), :]
        dst = (o, dq, lk, lv)[n].at[0, :, cols]
        return pltpu.make_async_copy(src, dst, out_own.at[n])

    def own_c():
        return pltpu.make_async_copy(xc.at[me], xl.at[head], out_own.at[4])

    @pl.when(mine)
    def _():
        for n in range(4):
            own_in(n).start()
        own_row().start()

    lax.fori_loop(1, SEQ, send_row, 0)
    lax.fori_loop(1, SEQ, send_kv, 0)

    @pl.when(mine)
    def _():
        remote(xin.at[pl.ds(0, SEQ - 1)], xin.at[pl.ds(0, SEQ - 1)], r_send, r_recv, (sh, me)).wait_recv()
        own_row().wait()
        dst = pl.ds(pl.multiple_of(OWN + sh * SEQ, SEQ), SEQ)
        for n, buf in enumerate((kx, vx)):
            rows = xin[:, n, :].astype(BF16)
            xs[n] = rows
            buf[dst, :] = rows

        def send_x(j, _):
            to = sibling(j)
            remote(xs.at[0], kx.at[dst, :], x_send.at[0], x_recv.at[0], to).start()
            remote(xs.at[1], vx.at[dst, :], x_send.at[1], x_recv.at[1], to).start()
            return 0

        lax.fori_loop(1, SHOTS, send_x, 0)

    lax.fori_loop(1, SEQ, send_qg, 0)

    @pl.when(mine)
    def _():
        length = lens[sh]
        here = (sh, me)
        row = lax.broadcasted_iota(I32, (ROWS, D), 0)
        lane = lax.broadcasted_iota(I32, (ROWS, D), 1)
        for b in range(SEQ):
            alive = jnp.logical_or(row + b * ROWS < length, row + b * ROWS == pos[0, b])
            dead = jnp.logical_and(jnp.logical_not(alive), lane == 0)
            kb[b * ROWS : (b + 1) * ROWS, :] = jnp.where(dead, MASKED, 0.0).astype(BF16)
        for b in range(CROSS // ROWS):
            dead = jnp.logical_and((row + b * ROWS) // SEQ == sh, lane == 0)
            kb[OWN + b * ROWS : OWN + (b + 1) * ROWS, :] = jnp.where(dead, MASKED, 0.0).astype(BF16)
        vt[D : D + 16, :] = jnp.ones((16, KEYS), BF16)
        for n, buf in enumerate((kx, vx)):
            part = buf.at[pl.ds(0, OWN - ROWS), :]
            remote(part, part, in_send.at[n], kv_recv.at[n], here).wait_recv()
            own_in(n).wait()

        def turn(c, _):
            kt[:, at256(c)] = kx[at256(c), :].T
            vt[0:D, at256(c)] = vx[at256(c), :].T
            return 0

        lax.fori_loop(0, OWN // 256, turn, 0)
        for n, buf in enumerate((kx, vx)):
            part = buf.at[pl.ds(OWN, CROSS - SEQ), :]
            remote(part, part, x_send.at[n], x_recv.at[n], here).wait()
        lax.fori_loop(OWN // 256, KEYS // 256, turn, 0)

        def step(i, _):
            for n, (buf, sem) in enumerate(((qx, q_recv), (gx, g_recv))):

                @pl.when(i == 0)
                def _(n=n, buf=buf, sem=sem):
                    part = buf.at[at128(1 - x), :]
                    remote(part, part, in_send.at[2 + n], sem.at[i], here).wait_recv()
                    own_in(2 + n).wait()

                @pl.when(i > 0)
                def _(n=n, buf=buf, sem=sem):
                    part = buf.at[at256(i), :]
                    remote(part, part, in_send.at[2 + n], sem.at[i], here).wait_recv()

            attend(i, kx, vx, kb, qx, gx, kt, vt, logit, prob, dlog, gn, ox, dqx)
            cols = at128(head)
            for d in range(2):
                xt = (x + d) % 2
                to = (sh, 2 * ((z + zstep(i) + 8) % 8) + xt)
                slot = at128(2 * i + xt)

                def start(slot=slot, to=to):
                    remote(ox.at[slot, :], o.at[0, :, cols], out_send.at[0], out_recv.at[0], to).start()
                    remote(dqx.at[slot, :], dq.at[0, :, cols], out_send.at[1], out_recv.at[1], to).start()

                if d == 1:
                    start()
                else:
                    pl.when(i > 0)(start)

                    @pl.when(i == 0)
                    def _():
                        own_out(0).start()
                        own_out(1).start()

            return 0

        lax.fori_loop(0, SEQ // 2, step, 0)

        cross = pl.ds(OWN, CROSS)
        xg[:, 0:SEQ, :] = (nn(dlog[cross, :], qx[...]) * SCALE).reshape(SHOTS, SEQ, D)
        xg[:, SEQ : 2 * SEQ, :] = nn(prob[cross, :], gn[...]).reshape(SHOTS, SEQ, D)
        xr[pl.ds(sh, 1)] = jnp.zeros((1, 2 * SEQ, D), F32)

        def send_g(j, _):
            s = (sh + j) % SHOTS
            remote(xg.at[s], xr.at[sh], x_send.at[2], x_recv.at[2], sibling(j)).start()
            return 0

        lax.fori_loop(1, SHOTS, send_g, 0)

        def send_c(j, _):
            t = (me + j) % SEQ
            remote(xc.at[t], xl.at[head], c_send, c_recv, (sh, t)).start()
            return 0

        def close():
            part = xr.at[pl.ds(0, SHOTS - 1)]
            remote(part, part, x_send.at[2], x_recv.at[2], here).wait()
            total = jnp.sum(xr[...], axis=0)
            xc[...] = jnp.zeros_like(xc)
            for b in range(SEQ):
                xc[b, 0:1, :] = total[b : b + 1, :]
                xc[b, 1:2, :] = total[SEQ + b : SEQ + b + 1, :]
            own_c().start()
            lax.fori_loop(1, SEQ, send_c, 0)

        def finish(i, _):
            pl.when(i == CLOSE)(close)
            zt = (z + zstep(i) + 8) % 8
            rows = at256(zt)
            cols = at128(head)
            dkx[rows, :] = (nn(dlog[rows, :], qx[...]) * SCALE).astype(BF16)
            dvx[rows, :] = nn(prob[rows, :], gn[...]).astype(BF16)
            for d in range(2):
                t = 2 * zt + (x + d) % 2

                def start(t=t):
                    remote(dkx.at[at128(t), :], lk.at[0, :, cols], out_send.at[2], out_recv.at[2], (sh, t)).start()
                    remote(dvx.at[at128(t), :], lv.at[0, :, cols], out_send.at[3], out_recv.at[3], (sh, t)).start()

                if d == 1:
                    start()
                else:
                    pl.when(i > 0)(start)

                    @pl.when(i == 0)
                    def _():
                        own_out(2).start()
                        own_out(3).start()

            return 0

        lax.fori_loop(0, SEQ // 2, finish, 0)

        for n, buf in enumerate((ox, dqx, dkx, dvx)):
            part = buf.at[pl.ds(0, OWN - ROWS), :]
            remote(part, part, out_send.at[n], out_recv.at[n], here).wait_send()
            own_out(n).wait()
        own_c().wait()
        part = xc.at[pl.ds(0, SEQ - 1)]
        remote(part, part, c_send, c_recv, here).wait_send()

    def settle(count):
        here = (sh, me)
        part = xl.at[pl.ds(0, count)]
        remote(part, part, c_send, c_recv, here).wait_recv()
        for n, buf in enumerate((o, dq, lk, lv)):
            part = buf.at[0, :, pl.ds(0, count * D)]
            remote(part, part, out_send.at[n], out_recv.at[n], here).wait_recv()
        part = rowt.at[:, pl.ds(0, count * D)]
        remote(part, part, r_send, r_recv, here).wait_send()
        for n, buf in enumerate((k, v, q, g)):
            part = buf.at[0, :, pl.ds(0, count * D)]
            remote(part, part, in_send.at[n], out_recv.at[n], here).wait_send()

    @pl.when(mine)
    def _():
        settle(HEADS - 1)

    @pl.when(jnp.logical_not(mine))
    def _():
        settle(HEADS)


def hand_over(pos_hbm, o, dq, lk, lv, xl_hbm, o_out, dq_out, dk_out, dv_out, pos, xl, bufs, come, go):
    small = [
        pltpu.make_async_copy(pos_hbm, pos, come.at[4]),
        pltpu.make_async_copy(xl_hbm, xl, come.at[5]),
    ]
    into = [pltpu.make_async_copy(ref, bufs.at[n], come.at[n]) for n, ref in enumerate((lk, lv, o, dq))]
    out = [pltpu.make_async_copy(bufs.at[n], ref, go.at[n]) for n, ref in enumerate((dk_out, dv_out, o_out, dq_out))]
    for copy in small + into:
        copy.start()
    for copy in small:
        copy.wait()
    me = lax.axis_index("seq")
    there = lax.broadcasted_iota(I32, (ROWS, D), 0) == pos[0, me] - me * ROWS
    for n in range(4):
        into[n].wait()
        if n < 2:
            for h in range(HEADS):
                cols = slice(h * D, (h + 1) * D)
                add = jnp.where(there, xl[h][n : n + 1, :], 0.0)
                bufs[n, 0, :, cols] = (bufs[n, 0, :, cols].astype(F32) + add).astype(BF16)
        out[n].start()
    for copy in out:
        copy.wait()


def body(query_rows, key_rows, value_rows, out_grad, shot_lengths, global_positions):
    hbm = pl.BlockSpec(memory_space=pltpu.HBM)
    shape = jax.ShapeDtypeStruct(query_rows.shape, BF16)
    dma = pltpu.SemaphoreType.DMA
    results = pl.pallas_call(
        kernel,
        out_shape=(shape,) * 4 + (jax.ShapeDtypeStruct((HEADS, 8, D), F32),),
        in_specs=[hbm] * 6,
        out_specs=(hbm,) * 5,
        scratch_shapes=[
            pltpu.SMEM((SHOTS,), I32),
            pltpu.SMEM((1, SEQ), I32),
            pltpu.VMEM((KEYS, D), BF16),
            pltpu.VMEM((KEYS, D), BF16),
            pltpu.VMEM((KEYS, D), BF16),
            pltpu.VMEM((OWN, D), BF16),
            pltpu.VMEM((OWN, D), BF16),
            pltpu.VMEM((D, KEYS), BF16),
            pltpu.VMEM((D + 16, KEYS), BF16),
            pltpu.VMEM((KEYS, QB), F32),
            pltpu.VMEM((KEYS, OWN), BF16),
            pltpu.VMEM((KEYS, OWN), BF16),
            pltpu.VMEM((OWN, D), BF16),
            pltpu.VMEM((OWN, D), BF16),
            pltpu.VMEM((OWN, D), BF16),
            pltpu.VMEM((OWN, D), BF16),
            pltpu.VMEM((OWN, D), BF16),
            pltpu.VMEM((ROWS, HEADS * D), BF16),
            pltpu.VMEM((ROWS, HEADS * D), BF16),
            pltpu.VMEM((8, HEADS * D), F32),
            pltpu.VMEM((SEQ, 8, D), F32),
            pltpu.VMEM((2, SEQ, D), BF16),
            pltpu.VMEM((SHOTS, 2 * SEQ, D), F32),
            pltpu.VMEM((SHOTS, 2 * SEQ, D), F32),
            pltpu.VMEM((SEQ, 8, D), F32),
            dma((4,)),
            dma((2,)),
            dma((SEQ // 2,)),
            dma((SEQ // 2,)),
            dma((5,)),
            dma((3,)),
            dma((3,)),
            dma((4,)),
            dma((4,)),
            dma((5,)),
            dma,
            dma,
            dma((4,)),
            dma,
            dma,
        ],
        compiler_params=pltpu.CompilerParams(
            collective_id=0, has_side_effects=True, vmem_limit_bytes=63 << 20
        ),
    )(shot_lengths, global_positions, query_rows, key_rows, value_rows, out_grad)
    return pl.pallas_call(
        hand_over,
        out_shape=(shape,) * 4,
        in_specs=[hbm] * 6,
        out_specs=(hbm,) * 4,
        scratch_shapes=[
            pltpu.SMEM((1, SEQ), I32),
            pltpu.VMEM((HEADS, 8, D), F32),
            pltpu.VMEM((4, 1, ROWS, HEADS * D), BF16),
            dma((6,)),
            dma((4,)),
        ],
        compiler_params=pltpu.CompilerParams(vmem_limit_bytes=63 << 20),
    )(global_positions, *results)


def solution(mesh):
    rows = P("shot", "seq", None)
    return jax.shard_map(
        body,
        mesh=mesh,
        in_specs=(rows, rows, rows, rows, P(), P("shot", None)),
        out_specs=(rows,) * 4,
        check_vma=False,
    )
```

```python
import math

import jax
import jax.numpy as jnp
from jax import lax
from jax.experimental import pallas as pl
from jax.experimental.pallas import tpu as pltpu
from jax.sharding import PartitionSpec as P

MESH = pl.DeviceIdType.MESH
F32, BF16, I32 = jnp.float32, jnp.bfloat16, jnp.int32
HEADS, D = 12, 128
SEQ, SHOTS = 16, 16
ROWS = 128
OWN = SEQ * ROWS
CROSS = SHOTS * SEQ
KEYS = OWN + CROSS
QB = 256
KC = 768
SCALE = 1.0 / math.sqrt(D)
LOGIT2 = SCALE * math.log2(math.e)
MASKED = -1e30
CLOSE = 4
IDLE = ((1, 4, 11, 14), (3, 6, 9, 12))


def nt(a, b):
    return lax.dot_general(a, b, (((1,), (1,)), ((), ())), preferred_element_type=F32)


def nn(a, b):
    return jnp.dot(a, b, preferred_element_type=F32)


def zstep(i):
    return ((i + 1) // 2) * (2 * (i % 2) - 1)


def idle(shot):
    core = shot % 2
    return tuple(a + core * (b - a) for a, b in zip(*IDLE))


def owns(t, shot):
    found = t >= 0
    for s in idle(shot):
        found = jnp.logical_and(found, t != s)
    return found


def head_of(t, shot):
    return t - sum((t - s + 15) // 16 for s in idle(shot))


def owner_of(h, shot):
    return h + sum((h + n - s + 16) // 16 for n, s in enumerate(idle(shot)))


def at128(i):
    return pl.ds(pl.multiple_of(i * 128, 128), 128)


def at256(i):
    return pl.ds(pl.multiple_of(i * 256, 256), 256)


def attend(i, kx, vx, kb, qx, gx, kt, vt, logit, prob, dlog, gn, ox, dqx):
    rows = at256(i)
    q = qx[rows, :]
    g = gx[rows, :]
    qa = jnp.concatenate([q, jnp.ones((QB, D), BF16)], 1)
    top = None
    for c in range(KEYS // KC):
        ks = slice(c * KC, (c + 1) * KC)
        s = nt(jnp.concatenate([kx[ks, :], kb[ks, :]], 1), qa)
        logit[ks, :] = s
        m = jnp.max(s.reshape(KC // 8, 8, QB), axis=0)
        top = m if top is None else jnp.maximum(top, m)
    top = jnp.max(top, axis=0, keepdims=True) * LOGIT2
    acc = None
    for c in range(KEYS // KC):
        ks = slice(c * KC, (c + 1) * KC)
        p = jnp.exp2(logit[ks, :] * LOGIT2 - top).astype(BF16)
        prob[ks, rows] = p
        part = nn(vt[:, ks], p)
        acc = part if acc is None else acc + part
    total = jnp.broadcast_to(acc[128:129, :], (D, QB))
    both = jnp.concatenate([acc[:128], total], 0).T
    inv = 1.0 / both[:, 128:]
    att = (both[:, :128] * inv).astype(BF16)
    ox[rows, :] = att
    gf = g.astype(F32)
    delta = jnp.sum(gf * att.astype(F32), axis=1, keepdims=True) * inv
    gs = (gf * inv).astype(BF16)
    gn[rows, :] = gs
    high = delta.astype(BF16).astype(F32)
    lane = lax.broadcasted_iota(I32, (QB, D), 1)
    tail = jnp.where(lane == 0, high, jnp.where(lane == 1, delta - high, 0.0))
    ga = jnp.concatenate([gs, tail.astype(BF16)], 1)
    lane = lax.broadcasted_iota(I32, (KC, D), 1)
    minus = jnp.where(lane < 2, -1.0, 0.0).astype(BF16)
    acc = None
    for c in range(KEYS // KC):
        ks = slice(c * KC, (c + 1) * KC)
        dp = nt(jnp.concatenate([vx[ks, :], minus], 1), ga)
        ds = prob[ks, rows] * dp.astype(BF16)
        dlog[ks, rows] = ds
        part = nn(kt[:, ks], ds)
        acc = part if acc is None else acc + part
    dqx[rows, :] = (acc * SCALE).T.astype(BF16)


def kernel(
    lens_hbm, pos_hbm, q, k, v, g, o, dq, lk, lv, xl, lens, pos,
    kx, vx, kb, qx, gx, kt, vt, logit, prob, dlog, gn, ox, dqx, dkx, dvx,
    kin, vin, rowt, xin, xs, xg, xr, xc,
    in_send, kv_recv, q_recv, g_recv, in_own, x_send, x_recv, out_send, out_recv, out_own, c_send, c_recv, s_own, r_send, r_recv,
):
    me, sh = lax.axis_index("seq"), lax.axis_index("shot")
    z, x = me // 2, me % 2
    mine = owns(me, sh)
    head = head_of(me, sh)

    scalars = [
        pltpu.make_async_copy(lens_hbm, lens, s_own.at[0]),
        pltpu.make_async_copy(pos_hbm, pos, s_own.at[1]),
    ]
    whole = [
        pltpu.make_async_copy(k.at[0], kin, s_own.at[2]),
        pltpu.make_async_copy(v.at[0], vin, s_own.at[3]),
    ]
    for copy in scalars + whole:
        copy.start()
    barrier = pltpu.get_barrier_semaphore()

    def greet(j, _):
        pl.semaphore_signal(barrier, inc=1, device_id=(sh, (me + j) % SEQ), device_id_type=MESH)
        return 0

    def sibling(j):
        s = (sh + j) % SHOTS
        return (s, owner_of(head, s))

    def greet_sibling(j, _):
        pl.semaphore_signal(barrier, inc=1, device_id=sibling(j), device_id_type=MESH)
        return 0

    lax.fori_loop(1, SEQ, greet, 0)

    @pl.when(mine)
    def _():
        lax.fori_loop(1, SHOTS, greet_sibling, 0)

    for copy in scalars + whole:
        copy.wait()
    chosen = lax.broadcasted_iota(I32, (8, ROWS), 1) == pos[0, me] - me * ROWS
    sub = lax.broadcasted_iota(I32, (8, ROWS), 0)
    first = jnp.where(jnp.logical_and(chosen, sub == 0), 1.0, 0.0).astype(BF16)
    second = jnp.where(jnp.logical_and(chosen, sub == 1), 1.0, 0.0).astype(BF16)
    rowt[...] = nn(first, kin[...]) + nn(second, vin[...])

    @pl.when(mine)
    def _():
        pl.semaphore_wait(barrier, SEQ + SHOTS - 2)

    @pl.when(jnp.logical_not(mine))
    def _():
        pl.semaphore_wait(barrier, SEQ - 1)

    def remote(src, dst, send, recv, to):
        return pltpu.make_async_remote_copy(
            src_ref=src, dst_ref=dst, send_sem=send, recv_sem=recv, device_id=to, device_id_type=MESH
        )

    def partner(j):
        return 2 * ((z - zstep(j // 2) + 8) % 8) + (x + j) % 2

    def send_row(j, _):
        t = partner(j)

        @pl.when(owns(t, sh))
        def _():
            cols = at128(head_of(t, sh))
            remote(rowt.at[:, cols], xin.at[me], r_send, r_recv, (sh, t)).start()

        return 0

    def own_row():
        return pltpu.make_async_copy(rowt.at[:, at128(head)], xin.at[me], in_own.at[4])

    def send_kv(j, _):
        t = partner(j)

        @pl.when(owns(t, sh))
        def _():
            cols = at128(head_of(t, sh))
            remote(k.at[0, :, cols], kx.at[at128(me), :], in_send.at[0], kv_recv.at[0], (sh, t)).start()
            remote(v.at[0, :, cols], vx.at[at128(me), :], in_send.at[1], kv_recv.at[1], (sh, t)).start()

        return 0

    def send_qg(j, _):
        t = partner(j)
        i = j // 2

        @pl.when(owns(t, sh))
        def _():
            cols = at128(head_of(t, sh))
            slot = at128(2 * i + x)
            remote(q.at[0, :, cols], qx.at[slot, :], in_send.at[2], q_recv.at[i], (sh, t)).start()
            remote(g.at[0, :, cols], gx.at[slot, :], in_send.at[3], g_recv.at[i], (sh, t)).start()

        return 0

    def own_in(n):
        cols = at128(head)
        src = (k, v, q, g)[n].at[0, :, cols]
        dst = (kx, vx, qx, gx)[n].at[at128(me if n < 2 else x), :]
        return pltpu.make_async_copy(src, dst, in_own.at[n])

    def own_out(n):
        cols = at128(head)
        src = (ox, dqx, dkx, dvx)[n].at[at128(x if n < 2 else me), :]
        dst = (o, dq, lk, lv)[n].at[0, :, cols]
        return pltpu.make_async_copy(src, dst, out_own.at[n])

    def own_c():
        return pltpu.make_async_copy(xc.at[me], xl.at[head], out_own.at[4])

    @pl.when(mine)
    def _():
        for n in range(4):
            own_in(n).start()
        own_row().start()

    lax.fori_loop(1, SEQ, send_row, 0)
    lax.fori_loop(1, SEQ, send_kv, 0)

    @pl.when(mine)
    def _():
        remote(xin.at[pl.ds(0, SEQ - 1)], xin.at[pl.ds(0, SEQ - 1)], r_send, r_recv, (sh, me)).wait_recv()
        own_row().wait()
        dst = pl.ds(pl.multiple_of(OWN + sh * SEQ, SEQ), SEQ)
        for n, buf in enumerate((kx, vx)):
            rows = xin[:, n, :].astype(BF16)
            xs[n] = rows
            buf[dst, :] = rows

        def send_x(j, _):
            to = sibling(j)
            remote(xs.at[0], kx.at[dst, :], x_send.at[0], x_recv.at[0], to).start()
            remote(xs.at[1], vx.at[dst, :], x_send.at[1], x_recv.at[1], to).start()
            return 0

        lax.fori_loop(1, SHOTS, send_x, 0)

    lax.fori_loop(1, SEQ, send_qg, 0)

    @pl.when(mine)
    def _():
        length = lens[sh]
        here = (sh, me)
        row = lax.broadcasted_iota(I32, (ROWS, D), 0)
        lane = lax.broadcasted_iota(I32, (ROWS, D), 1)
        for b in range(SEQ):
            alive = jnp.logical_or(row + b * ROWS < length, row + b * ROWS == pos[0, b])
            dead = jnp.logical_and(jnp.logical_not(alive), lane == 0)
            kb[b * ROWS : (b + 1) * ROWS, :] = jnp.where(dead, MASKED, 0.0).astype(BF16)
        for b in range(CROSS // ROWS):
            dead = jnp.logical_and((row + b * ROWS) // SEQ == sh, lane == 0)
            kb[OWN + b * ROWS : OWN + (b + 1) * ROWS, :] = jnp.where(dead, MASKED, 0.0).astype(BF16)
        vt[D : D + 16, :] = jnp.ones((16, KEYS), BF16)
        for n, buf in enumerate((kx, vx)):
            part = buf.at[pl.ds(0, OWN - ROWS), :]
            remote(part, part, in_send.at[n], kv_recv.at[n], here).wait_recv()
            own_in(n).wait()

        def turn(c, _):
            kt[:, at256(c)] = kx[at256(c), :].T
            vt[0:D, at256(c)] = vx[at256(c), :].T
            return 0

        lax.fori_loop(0, OWN // 256, turn, 0)
        for n, buf in enumerate((kx, vx)):
            part = buf.at[pl.ds(OWN, CROSS - SEQ), :]
            remote(part, part, x_send.at[n], x_recv.at[n], here).wait()
        lax.fori_loop(OWN // 256, KEYS // 256, turn, 0)

        def step(i, _):
            for n, (buf, sem) in enumerate(((qx, q_recv), (gx, g_recv))):

                @pl.when(i == 0)
                def _(n=n, buf=buf, sem=sem):
                    part = buf.at[at128(1 - x), :]
                    remote(part, part, in_send.at[2 + n], sem.at[i], here).wait_recv()
                    own_in(2 + n).wait()

                @pl.when(i > 0)
                def _(n=n, buf=buf, sem=sem):
                    part = buf.at[at256(i), :]
                    remote(part, part, in_send.at[2 + n], sem.at[i], here).wait_recv()

            attend(i, kx, vx, kb, qx, gx, kt, vt, logit, prob, dlog, gn, ox, dqx)
            cols = at128(head)
            for d in range(2):
                xt = (x + d) % 2
                to = (sh, 2 * ((z + zstep(i) + 8) % 8) + xt)
                slot = at128(2 * i + xt)

                def start(slot=slot, to=to):
                    remote(ox.at[slot, :], o.at[0, :, cols], out_send.at[0], out_recv.at[0], to).start()
                    remote(dqx.at[slot, :], dq.at[0, :, cols], out_send.at[1], out_recv.at[1], to).start()

                if d == 1:
                    start()
                else:
                    pl.when(i > 0)(start)

                    @pl.when(i == 0)
                    def _():
                        own_out(0).start()
                        own_out(1).start()

            return 0

        lax.fori_loop(0, SEQ // 2, step, 0)

        cross = pl.ds(OWN, CROSS)
        xg[:, 0:SEQ, :] = (nn(dlog[cross, :], qx[...]) * SCALE).reshape(SHOTS, SEQ, D)
        xg[:, SEQ : 2 * SEQ, :] = nn(prob[cross, :], gn[...]).reshape(SHOTS, SEQ, D)
        xr[pl.ds(sh, 1)] = jnp.zeros((1, 2 * SEQ, D), F32)

        def send_g(j, _):
            s = (sh + j) % SHOTS
            remote(xg.at[s], xr.at[sh], x_send.at[2], x_recv.at[2], sibling(j)).start()
            return 0

        lax.fori_loop(1, SHOTS, send_g, 0)

        def send_c(j, _):
            t = (me + j) % SEQ
            remote(xc.at[t], xl.at[head], c_send, c_recv, (sh, t)).start()
            return 0

        def close():
            part = xr.at[pl.ds(0, SHOTS - 1)]
            remote(part, part, x_send.at[2], x_recv.at[2], here).wait()
            total = jnp.sum(xr[...], axis=0)
            xc[...] = jnp.zeros_like(xc)
            for b in range(SEQ):
                xc[b, 0:1, :] = total[b : b + 1, :]
                xc[b, 1:2, :] = total[SEQ + b : SEQ + b + 1, :]
            own_c().start()
            lax.fori_loop(1, SEQ, send_c, 0)

        def finish(i, _):
            pl.when(i == CLOSE)(close)
            zt = (z + zstep(i) + 8) % 8
            rows = at256(zt)
            cols = at128(head)
            dkx[rows, :] = (nn(dlog[rows, :], qx[...]) * SCALE).astype(BF16)
            dvx[rows, :] = nn(prob[rows, :], gn[...]).astype(BF16)
            for d in range(2):
                t = 2 * zt + (x + d) % 2

                def start(t=t):
                    remote(dkx.at[at128(t), :], lk.at[0, :, cols], out_send.at[2], out_recv.at[2], (sh, t)).start()
                    remote(dvx.at[at128(t), :], lv.at[0, :, cols], out_send.at[3], out_recv.at[3], (sh, t)).start()

                if d == 1:
                    start()
                else:
                    pl.when(i > 0)(start)

                    @pl.when(i == 0)
                    def _():
                        own_out(2).start()
                        own_out(3).start()

            return 0

        lax.fori_loop(0, SEQ // 2, finish, 0)

        for n, buf in enumerate((ox, dqx, dkx, dvx)):
            part = buf.at[pl.ds(0, OWN - ROWS), :]
            remote(part, part, out_send.at[n], out_recv.at[n], here).wait_send()
            own_out(n).wait()
        own_c().wait()
        part = xc.at[pl.ds(0, SEQ - 1)]
        remote(part, part, c_send, c_recv, here).wait_send()

    def settle(count):
        here = (sh, me)
        part = xl.at[pl.ds(0, count)]
        remote(part, part, c_send, c_recv, here).wait_recv()
        for n, buf in enumerate((o, dq, lk, lv)):
            part = buf.at[0, :, pl.ds(0, count * D)]
            remote(part, part, out_send.at[n], out_recv.at[n], here).wait_recv()
        part = rowt.at[:, pl.ds(0, count * D)]
        remote(part, part, r_send, r_recv, here).wait_send()
        for n, buf in enumerate((k, v, q, g)):
            part = buf.at[0, :, pl.ds(0, count * D)]
            remote(part, part, in_send.at[n], out_recv.at[n], here).wait_send()

    @pl.when(mine)
    def _():
        settle(HEADS - 1)

    @pl.when(jnp.logical_not(mine))
    def _():
        settle(HEADS)


def hand_over(pos_hbm, o, dq, lk, lv, xl_hbm, o_out, dq_out, dk_out, dv_out, pos, xl, bufs, come, go):
    small = [
        pltpu.make_async_copy(pos_hbm, pos, come.at[4]),
        pltpu.make_async_copy(xl_hbm, xl, come.at[5]),
    ]
    into = [pltpu.make_async_copy(ref, bufs.at[n], come.at[n]) for n, ref in enumerate((lk, lv, o, dq))]
    out = [pltpu.make_async_copy(bufs.at[n], ref, go.at[n]) for n, ref in enumerate((dk_out, dv_out, o_out, dq_out))]
    for copy in small + into:
        copy.start()
    for copy in small:
        copy.wait()
    me = lax.axis_index("seq")
    there = lax.broadcasted_iota(I32, (ROWS, D), 0) == pos[0, me] - me * ROWS
    for n in range(4):
        into[n].wait()
        if n < 2:
            for h in range(HEADS):
                cols = slice(h * D, (h + 1) * D)
                add = jnp.where(there, xl[h][n : n + 1, :], 0.0)
                bufs[n, 0, :, cols] = (bufs[n, 0, :, cols].astype(F32) + add).astype(BF16)
        out[n].start()
    for copy in out:
        copy.wait()


def body(query_rows, key_rows, value_rows, out_grad, shot_lengths, global_positions):
    hbm = pl.BlockSpec(memory_space=pltpu.HBM)
    shape = jax.ShapeDtypeStruct(query_rows.shape, BF16)
    dma = pltpu.SemaphoreType.DMA
    results = pl.pallas_call(
        kernel,
        out_shape=(shape,) * 4 + (jax.ShapeDtypeStruct((HEADS, 8, D), F32),),
        in_specs=[hbm] * 6,
        out_specs=(hbm,) * 5,
        scratch_shapes=[
            pltpu.SMEM((SHOTS,), I32),
            pltpu.SMEM((1, SEQ), I32),
            pltpu.VMEM((KEYS, D), BF16),
            pltpu.VMEM((KEYS, D), BF16),
            pltpu.VMEM((KEYS, D), BF16),
            pltpu.VMEM((OWN, D), BF16),
            pltpu.VMEM((OWN, D), BF16),
            pltpu.VMEM((D, KEYS), BF16),
            pltpu.VMEM((D + 16, KEYS), BF16),
            pltpu.VMEM((KEYS, QB), F32),
            pltpu.VMEM((KEYS, OWN), BF16),
            pltpu.VMEM((KEYS, OWN), BF16),
            pltpu.VMEM((OWN, D), BF16),
            pltpu.VMEM((OWN, D), BF16),
            pltpu.VMEM((OWN, D), BF16),
            pltpu.VMEM((OWN, D), BF16),
            pltpu.VMEM((OWN, D), BF16),
            pltpu.VMEM((ROWS, HEADS * D), BF16),
            pltpu.VMEM((ROWS, HEADS * D), BF16),
            pltpu.VMEM((8, HEADS * D), F32),
            pltpu.VMEM((SEQ, 8, D), F32),
            pltpu.VMEM((2, SEQ, D), BF16),
            pltpu.VMEM((SHOTS, 2 * SEQ, D), F32),
            pltpu.VMEM((SHOTS, 2 * SEQ, D), F32),
            pltpu.VMEM((SEQ, 8, D), F32),
            dma((4,)),
            dma((2,)),
            dma((SEQ // 2,)),
            dma((SEQ // 2,)),
            dma((5,)),
            dma((3,)),
            dma((3,)),
            dma((4,)),
            dma((4,)),
            dma((5,)),
            dma,
            dma,
            dma((4,)),
            dma,
            dma,
        ],
        compiler_params=pltpu.CompilerParams(
            collective_id=0, has_side_effects=True, vmem_limit_bytes=63 << 20
        ),
    )(shot_lengths, global_positions, query_rows, key_rows, value_rows, out_grad)
    return pl.pallas_call(
        hand_over,
        out_shape=(shape,) * 4,
        in_specs=[hbm] * 6,
        out_specs=(hbm,) * 4,
        scratch_shapes=[
            pltpu.SMEM((1, SEQ), I32),
            pltpu.VMEM((HEADS, 8, D), F32),
            pltpu.VMEM((4, 1, ROWS, HEADS * D), BF16),
            dma((6,)),
            dma((4,)),
        ],
        compiler_params=pltpu.CompilerParams(vmem_limit_bytes=63 << 20),
    )(global_positions, *results)


def solution(mesh):
    rows = P("shot", "seq", None)
    return jax.shard_map(
        body,
        mesh=mesh,
        in_specs=(rows, rows, rows, rows, P(), P("shot", None)),
        out_specs=(rows,) * 4,
        check_vma=False,
    )
```

```python
import math

import jax
import jax.numpy as jnp
from jax import lax
from jax.experimental import pallas as pl
from jax.experimental.pallas import tpu as pltpu
from jax.sharding import PartitionSpec as P

MESH = pl.DeviceIdType.MESH
F32, BF16, I32 = jnp.float32, jnp.bfloat16, jnp.int32
HEADS, D = 12, 128
SEQ, SHOTS = 16, 16
ROWS = 128
OWN = SEQ * ROWS
CROSS = SHOTS * SEQ
KEYS = OWN + CROSS
QB = 256
KC = 768
SCALE = 1.0 / math.sqrt(D)
LOGIT2 = SCALE * math.log2(math.e)
MASKED = -1e30
CLOSE = 4
IDLE = ((1, 4, 11, 14), (3, 6, 9, 12))


def nt(a, b):
    return lax.dot_general(a, b, (((1,), (1,)), ((), ())), preferred_element_type=F32)


def nn(a, b):
    return jnp.dot(a, b, preferred_element_type=F32)


def zstep(i):
    return ((i + 1) // 2) * (2 * (i % 2) - 1)


def idle(shot):
    core = shot % 2
    return tuple(a + core * (b - a) for a, b in zip(*IDLE))


def owns(t, shot):
    found = t >= 0
    for s in idle(shot):
        found = jnp.logical_and(found, t != s)
    return found


def head_of(t, shot):
    return t - sum((t - s + 15) // 16 for s in idle(shot))


def owner_of(h, shot):
    return h + sum((h + n - s + 16) // 16 for n, s in enumerate(idle(shot)))


def at128(i):
    return pl.ds(pl.multiple_of(i * 128, 128), 128)


def at256(i):
    return pl.ds(pl.multiple_of(i * 256, 256), 256)


def attend(i, kx, vx, kb, qx, gx, kt, vt, logit, prob, dlog, gn, ox, dqx, send):
    rows = at256(i)
    q = qx[rows, :]
    g = gx[rows, :]
    qa = jnp.concatenate([q, jnp.ones((QB, D), BF16)], 1)
    top = None
    for c in range(KEYS // KC):
        ks = slice(c * KC, (c + 1) * KC)
        s = nt(jnp.concatenate([kx[ks, :], kb[ks, :]], 1), qa)
        logit[ks, :] = s
        m = jnp.max(s.reshape(KC // 8, 8, QB), axis=0)
        top = m if top is None else jnp.maximum(top, m)
    top = jnp.max(top, axis=0, keepdims=True) * LOGIT2
    acc = None
    for c in range(KEYS // KC):
        ks = slice(c * KC, (c + 1) * KC)
        p = jnp.exp2(logit[ks, :] * LOGIT2 - top).astype(BF16)
        prob[ks, rows] = p
        part = nn(vt[:, ks], p)
        acc = part if acc is None else acc + part
    total = jnp.broadcast_to(acc[128:129, :], (D, QB))
    both = jnp.concatenate([acc[:128], total], 0).T
    inv = 1.0 / both[:, 128:]
    att = (both[:, :128] * inv).astype(BF16)
    ox[rows, :] = att
    send(0)
    gf = g.astype(F32)
    delta = jnp.sum(gf * att.astype(F32), axis=1, keepdims=True) * inv
    gs = (gf * inv).astype(BF16)
    gn[rows, :] = gs
    high = delta.astype(BF16).astype(F32)
    lane = lax.broadcasted_iota(I32, (QB, D), 1)
    tail = jnp.where(lane == 0, high, jnp.where(lane == 1, delta - high, 0.0))
    ga = jnp.concatenate([gs, tail.astype(BF16)], 1)
    lane = lax.broadcasted_iota(I32, (KC, D), 1)
    minus = jnp.where(lane < 2, -1.0, 0.0).astype(BF16)
    acc = None
    for c in range(KEYS // KC):
        ks = slice(c * KC, (c + 1) * KC)
        dp = nt(jnp.concatenate([vx[ks, :], minus], 1), ga)
        ds = prob[ks, rows] * dp.astype(BF16)
        dlog[ks, rows] = ds
        part = nn(kt[:, ks], ds)
        acc = part if acc is None else acc + part
    dqx[rows, :] = (acc * SCALE).T.astype(BF16)
    send(1)


def kernel(
    lens_hbm, pos_hbm, q, k, v, g, o, dq, lk, lv, xl, lens, pos,
    kx, vx, kb, qx, gx, kt, vt, logit, prob, dlog, gn, ox, dqx, dkx, dvx,
    kin, vin, rowt, xin, xs, xg, xr, xc,
    in_send, kv_recv, q_recv, g_recv, in_own, x_send, x_recv, out_send, out_recv, out_own, c_send, c_recv, s_own, r_send, r_recv,
):
    me, sh = lax.axis_index("seq"), lax.axis_index("shot")
    z, x = me // 2, me % 2
    mine = owns(me, sh)
    head = head_of(me, sh)

    scalars = [
        pltpu.make_async_copy(lens_hbm, lens, s_own.at[0]),
        pltpu.make_async_copy(pos_hbm, pos, s_own.at[1]),
    ]
    whole = [
        pltpu.make_async_copy(k.at[0], kin, s_own.at[2]),
        pltpu.make_async_copy(v.at[0], vin, s_own.at[3]),
    ]
    for copy in scalars + whole:
        copy.start()
    barrier = pltpu.get_barrier_semaphore()

    def greet(j, _):
        pl.semaphore_signal(barrier, inc=1, device_id=(sh, (me + j) % SEQ), device_id_type=MESH)
        return 0

    def sibling(j):
        s = (sh + j) % SHOTS
        return (s, owner_of(head, s))

    def greet_sibling(j, _):
        pl.semaphore_signal(barrier, inc=1, device_id=sibling(j), device_id_type=MESH)
        return 0

    lax.fori_loop(1, SEQ, greet, 0)

    @pl.when(mine)
    def _():
        lax.fori_loop(1, SHOTS, greet_sibling, 0)

    for copy in scalars + whole:
        copy.wait()
    chosen = lax.broadcasted_iota(I32, (8, ROWS), 1) == pos[0, me] - me * ROWS
    sub = lax.broadcasted_iota(I32, (8, ROWS), 0)
    first = jnp.where(jnp.logical_and(chosen, sub == 0), 1.0, 0.0).astype(BF16)
    second = jnp.where(jnp.logical_and(chosen, sub == 1), 1.0, 0.0).astype(BF16)
    rowt[...] = nn(first, kin[...]) + nn(second, vin[...])

    @pl.when(mine)
    def _():
        pl.semaphore_wait(barrier, SEQ + SHOTS - 2)

    @pl.when(jnp.logical_not(mine))
    def _():
        pl.semaphore_wait(barrier, SEQ - 1)

    def remote(src, dst, send, recv, to):
        return pltpu.make_async_remote_copy(
            src_ref=src, dst_ref=dst, send_sem=send, recv_sem=recv, device_id=to, device_id_type=MESH
        )

    def partner(j):
        return 2 * ((z - zstep(j // 2) + 8) % 8) + (x + j) % 2

    def send_row(j, _):
        t = partner(j)

        @pl.when(owns(t, sh))
        def _():
            cols = at128(head_of(t, sh))
            remote(rowt.at[:, cols], xin.at[me], r_send, r_recv, (sh, t)).start()

        return 0

    def own_row():
        return pltpu.make_async_copy(rowt.at[:, at128(head)], xin.at[me], in_own.at[4])

    def send_kv(j, _):
        t = partner(j)

        @pl.when(owns(t, sh))
        def _():
            cols = at128(head_of(t, sh))
            remote(k.at[0, :, cols], kx.at[at128(me), :], in_send.at[0], kv_recv.at[0], (sh, t)).start()
            remote(v.at[0, :, cols], vx.at[at128(me), :], in_send.at[1], kv_recv.at[1], (sh, t)).start()

        return 0

    def send_qg(j, _):
        t = partner(j)
        i = j // 2

        @pl.when(owns(t, sh))
        def _():
            cols = at128(head_of(t, sh))
            slot = at128(2 * i + x)
            remote(q.at[0, :, cols], qx.at[slot, :], in_send.at[2], q_recv.at[i], (sh, t)).start()
            remote(g.at[0, :, cols], gx.at[slot, :], in_send.at[3], g_recv.at[i], (sh, t)).start()

        return 0

    def own_in(n):
        cols = at128(head)
        src = (k, v, q, g)[n].at[0, :, cols]
        dst = (kx, vx, qx, gx)[n].at[at128(me if n < 2 else x), :]
        return pltpu.make_async_copy(src, dst, in_own.at[n])

    def own_out(n):
        cols = at128(head)
        src = (ox, dqx, dkx, dvx)[n].at[at128(x if n < 2 else me), :]
        dst = (o, dq, lk, lv)[n].at[0, :, cols]
        return pltpu.make_async_copy(src, dst, out_own.at[n])

    def own_c():
        return pltpu.make_async_copy(xc.at[me], xl.at[head], out_own.at[4])

    @pl.when(mine)
    def _():
        for n in range(4):
            own_in(n).start()
        own_row().start()

    lax.fori_loop(1, SEQ, send_row, 0)
    lax.fori_loop(1, SEQ, send_kv, 0)

    @pl.when(mine)
    def _():
        remote(xin.at[pl.ds(0, SEQ - 1)], xin.at[pl.ds(0, SEQ - 1)], r_send, r_recv, (sh, me)).wait_recv()
        own_row().wait()
        dst = pl.ds(pl.multiple_of(OWN + sh * SEQ, SEQ), SEQ)
        for n, buf in enumerate((kx, vx)):
            rows = xin[:, n, :].astype(BF16)
            xs[n] = rows
            buf[dst, :] = rows

        def send_x(j, _):
            to = sibling(j)
            remote(xs.at[0], kx.at[dst, :], x_send.at[0], x_recv.at[0], to).start()
            remote(xs.at[1], vx.at[dst, :], x_send.at[1], x_recv.at[1], to).start()
            return 0

        lax.fori_loop(1, SHOTS, send_x, 0)

    lax.fori_loop(1, SEQ, send_qg, 0)

    @pl.when(mine)
    def _():
        length = lens[sh]
        here = (sh, me)
        row = lax.broadcasted_iota(I32, (ROWS, D), 0)
        lane = lax.broadcasted_iota(I32, (ROWS, D), 1)
        for b in range(SEQ):
            alive = jnp.logical_or(row + b * ROWS < length, row + b * ROWS == pos[0, b])
            dead = jnp.logical_and(jnp.logical_not(alive), lane == 0)
            kb[b * ROWS : (b + 1) * ROWS, :] = jnp.where(dead, MASKED, 0.0).astype(BF16)
        for b in range(CROSS // ROWS):
            dead = jnp.logical_and((row + b * ROWS) // SEQ == sh, lane == 0)
            kb[OWN + b * ROWS : OWN + (b + 1) * ROWS, :] = jnp.where(dead, MASKED, 0.0).astype(BF16)
        vt[D : D + 16, :] = jnp.ones((16, KEYS), BF16)
        for n, buf in enumerate((kx, vx)):
            part = buf.at[pl.ds(0, OWN - ROWS), :]
            remote(part, part, in_send.at[n], kv_recv.at[n], here).wait_recv()
            own_in(n).wait()

        def turn(c, _):
            kt[:, at256(c)] = kx[at256(c), :].T
            vt[0:D, at256(c)] = vx[at256(c), :].T
            return 0

        lax.fori_loop(0, OWN // 256, turn, 0)
        for n, buf in enumerate((kx, vx)):
            part = buf.at[pl.ds(OWN, CROSS - SEQ), :]
            remote(part, part, x_send.at[n], x_recv.at[n], here).wait()
        lax.fori_loop(OWN // 256, KEYS // 256, turn, 0)

        def step(i, _):
            for n, (buf, sem) in enumerate(((qx, q_recv), (gx, g_recv))):

                @pl.when(i == 0)
                def _(n=n, buf=buf, sem=sem):
                    part = buf.at[at128(1 - x), :]
                    remote(part, part, in_send.at[2 + n], sem.at[i], here).wait_recv()
                    own_in(2 + n).wait()

                @pl.when(i > 0)
                def _(n=n, buf=buf, sem=sem):
                    part = buf.at[at256(i), :]
                    remote(part, part, in_send.at[2 + n], sem.at[i], here).wait_recv()

            cols = at128(head)

            def send(n):
                src, dst = ((ox, o), (dqx, dq))[n]
                for d in range(2):
                    xt = (x + d) % 2
                    to = (sh, 2 * ((z + zstep(i) + 8) % 8) + xt)
                    slot = at128(2 * i + xt)

                    def start(slot=slot, to=to):
                        remote(src.at[slot, :], dst.at[0, :, cols], out_send.at[n], out_recv.at[n], to).start()

                    if d == 1:
                        start()
                    else:
                        pl.when(i > 0)(start)

                        @pl.when(i == 0)
                        def _():
                            own_out(n).start()

            attend(i, kx, vx, kb, qx, gx, kt, vt, logit, prob, dlog, gn, ox, dqx, send)
            return 0

        lax.fori_loop(0, SEQ // 2, step, 0)

        cross = pl.ds(OWN, CROSS)
        xg[:, 0:SEQ, :] = (nn(dlog[cross, :], qx[...]) * SCALE).reshape(SHOTS, SEQ, D)
        xg[:, SEQ : 2 * SEQ, :] = nn(prob[cross, :], gn[...]).reshape(SHOTS, SEQ, D)
        xr[pl.ds(sh, 1)] = jnp.zeros((1, 2 * SEQ, D), F32)

        def send_g(j, _):
            s = (sh + j) % SHOTS
            remote(xg.at[s], xr.at[sh], x_send.at[2], x_recv.at[2], sibling(j)).start()
            return 0

        lax.fori_loop(1, SHOTS, send_g, 0)

        def send_c(j, _):
            t = (me + j) % SEQ
            remote(xc.at[t], xl.at[head], c_send, c_recv, (sh, t)).start()
            return 0

        def close():
            part = xr.at[pl.ds(0, SHOTS - 1)]
            remote(part, part, x_send.at[2], x_recv.at[2], here).wait()
            total = jnp.sum(xr[...], axis=0)
            xc[...] = jnp.zeros_like(xc)
            for b in range(SEQ):
                xc[b, 0:1, :] = total[b : b + 1, :]
                xc[b, 1:2, :] = total[SEQ + b : SEQ + b + 1, :]
            own_c().start()
            lax.fori_loop(1, SEQ, send_c, 0)

        def finish(i, _):
            pl.when(i == CLOSE)(close)
            zt = (z + zstep(i) + 8) % 8
            rows = at256(zt)
            cols = at128(head)
            dkx[rows, :] = (nn(dlog[rows, :], qx[...]) * SCALE).astype(BF16)
            dvx[rows, :] = nn(prob[rows, :], gn[...]).astype(BF16)
            for d in range(2):
                t = 2 * zt + (x + d) % 2

                def start(t=t):
                    remote(dkx.at[at128(t), :], lk.at[0, :, cols], out_send.at[2], out_recv.at[2], (sh, t)).start()
                    remote(dvx.at[at128(t), :], lv.at[0, :, cols], out_send.at[3], out_recv.at[3], (sh, t)).start()

                if d == 1:
                    start()
                else:
                    pl.when(i > 0)(start)

                    @pl.when(i == 0)
                    def _():
                        own_out(2).start()
                        own_out(3).start()

            return 0

        lax.fori_loop(0, SEQ // 2, finish, 0)

        for n, buf in enumerate((ox, dqx, dkx, dvx)):
            part = buf.at[pl.ds(0, OWN - ROWS), :]
            remote(part, part, out_send.at[n], out_recv.at[n], here).wait_send()
            own_out(n).wait()
        own_c().wait()
        part = xc.at[pl.ds(0, SEQ - 1)]
        remote(part, part, c_send, c_recv, here).wait_send()

    def settle(count):
        here = (sh, me)
        part = xl.at[pl.ds(0, count)]
        remote(part, part, c_send, c_recv, here).wait_recv()
        for n, buf in enumerate((o, dq, lk, lv)):
            part = buf.at[0, :, pl.ds(0, count * D)]
            remote(part, part, out_send.at[n], out_recv.at[n], here).wait_recv()
        part = rowt.at[:, pl.ds(0, count * D)]
        remote(part, part, r_send, r_recv, here).wait_send()
        for n, buf in enumerate((k, v, q, g)):
            part = buf.at[0, :, pl.ds(0, count * D)]
            remote(part, part, in_send.at[n], out_recv.at[n], here).wait_send()

    @pl.when(mine)
    def _():
        settle(HEADS - 1)

    @pl.when(jnp.logical_not(mine))
    def _():
        settle(HEADS)


def hand_over(pos_hbm, o, dq, lk, lv, xl_hbm, o_out, dq_out, dk_out, dv_out, pos, xl, bufs, come, go):
    small = [
        pltpu.make_async_copy(pos_hbm, pos, come.at[4]),
        pltpu.make_async_copy(xl_hbm, xl, come.at[5]),
    ]
    into = [pltpu.make_async_copy(ref, bufs.at[n], come.at[n]) for n, ref in enumerate((lk, lv, o, dq))]
    out = [pltpu.make_async_copy(bufs.at[n], ref, go.at[n]) for n, ref in enumerate((dk_out, dv_out, o_out, dq_out))]
    for copy in small + into:
        copy.start()
    for copy in small:
        copy.wait()
    me = lax.axis_index("seq")
    there = lax.broadcasted_iota(I32, (ROWS, D), 0) == pos[0, me] - me * ROWS
    for n in range(4):
        into[n].wait()
        if n < 2:
            for h in range(HEADS):
                cols = slice(h * D, (h + 1) * D)
                add = jnp.where(there, xl[h][n : n + 1, :], 0.0)
                bufs[n, 0, :, cols] = (bufs[n, 0, :, cols].astype(F32) + add).astype(BF16)
        out[n].start()
    for copy in out:
        copy.wait()


def body(query_rows, key_rows, value_rows, out_grad, shot_lengths, global_positions):
    hbm = pl.BlockSpec(memory_space=pltpu.HBM)
    shape = jax.ShapeDtypeStruct(query_rows.shape, BF16)
    dma = pltpu.SemaphoreType.DMA
    results = pl.pallas_call(
        kernel,
        out_shape=(shape,) * 4 + (jax.ShapeDtypeStruct((HEADS, 8, D), F32),),
        in_specs=[hbm] * 6,
        out_specs=(hbm,) * 5,
        scratch_shapes=[
            pltpu.SMEM((SHOTS,), I32),
            pltpu.SMEM((1, SEQ), I32),
            pltpu.VMEM((KEYS, D), BF16),
            pltpu.VMEM((KEYS, D), BF16),
            pltpu.VMEM((KEYS, D), BF16),
            pltpu.VMEM((OWN, D), BF16),
            pltpu.VMEM((OWN, D), BF16),
            pltpu.VMEM((D, KEYS), BF16),
            pltpu.VMEM((D + 16, KEYS), BF16),
            pltpu.VMEM((KEYS, QB), F32),
            pltpu.VMEM((KEYS, OWN), BF16),
            pltpu.VMEM((KEYS, OWN), BF16),
            pltpu.VMEM((OWN, D), BF16),
            pltpu.VMEM((OWN, D), BF16),
            pltpu.VMEM((OWN, D), BF16),
            pltpu.VMEM((OWN, D), BF16),
            pltpu.VMEM((OWN, D), BF16),
            pltpu.VMEM((ROWS, HEADS * D), BF16),
            pltpu.VMEM((ROWS, HEADS * D), BF16),
            pltpu.VMEM((8, HEADS * D), F32),
            pltpu.VMEM((SEQ, 8, D), F32),
            pltpu.VMEM((2, SEQ, D), BF16),
            pltpu.VMEM((SHOTS, 2 * SEQ, D), F32),
            pltpu.VMEM((SHOTS, 2 * SEQ, D), F32),
            pltpu.VMEM((SEQ, 8, D), F32),
            dma((4,)),
            dma((2,)),
            dma((SEQ // 2,)),
            dma((SEQ // 2,)),
            dma((5,)),
            dma((3,)),
            dma((3,)),
            dma((4,)),
            dma((4,)),
            dma((5,)),
            dma,
            dma,
            dma((4,)),
            dma,
            dma,
        ],
        compiler_params=pltpu.CompilerParams(
            collective_id=0, has_side_effects=True, vmem_limit_bytes=63 << 20
        ),
    )(shot_lengths, global_positions, query_rows, key_rows, value_rows, out_grad)
    return pl.pallas_call(
        hand_over,
        out_shape=(shape,) * 4,
        in_specs=[hbm] * 6,
        out_specs=(hbm,) * 4,
        scratch_shapes=[
            pltpu.SMEM((1, SEQ), I32),
            pltpu.VMEM((HEADS, 8, D), F32),
            pltpu.VMEM((4, 1, ROWS, HEADS * D), BF16),
            dma((6,)),
            dma((4,)),
        ],
        compiler_params=pltpu.CompilerParams(vmem_limit_bytes=63 << 20),
    )(global_positions, *results)


def solution(mesh):
    rows = P("shot", "seq", None)
    return jax.shard_map(
        body,
        mesh=mesh,
        in_specs=(rows, rows, rows, rows, P(), P("shot", None)),
        out_specs=(rows,) * 4,
        check_vma=False,
    )
```
